128 devices in a mesh: cluster: 8 (over z_hi, y), cone: 16 (over z_lo, x, core).
Axes of the slice: x: 4, y: 4, z: 4 (z_hi: 2, z_lo: 2; z = z_hi * 2 + z_lo), core: 2. Of those that a mesh axis runs over, the one named last changes fastest.
Arguments:
- upper_coef: bfloat16 [256, 32, 128, 128], P('cluster', 'cone'), may hold values from -6 to 6
- phase: float32 [256, 32, 8], P('cluster', 'cone'), may hold values from -3.140625 to 3.140625
- cone_used: int32 [256, 32], P('cluster', 'cone'), may hold values 0 or 1
- transfer: bfloat16 [32, 8, 128, 128], P('cone'), may hold values from -0.5 to 0.5
- leaf_basis: bfloat16 [2048, 2, 256, 128], P(('cluster', 'cone')), may hold values from -0.09375 to 0.09375
- charges: bfloat16 [2048, 256, 256], P(('cluster', 'cone')), may hold values from -6 to 6
- neighbours: int32 [2048, 4], P(('cluster', 'cone')), may hold values from 0 to 2047, as said below
- near_real: bfloat16 [2048, 4, 256, 256], P(('cluster', 'cone')), may hold values from -0.1875 to 0.1875
- near_imag: bfloat16 [2048, 4, 256, 256], P(('cluster', 'cone')), may hold values from -0.1875 to 0.1875
Outputs:
- potential: bfloat16 [2048, 256, 256], P(('cluster', 'cone'))
The draws below stay inside these ranges and needn't reach their ends.
Inputs may be any that keep to these rules, and one draw needn't show every extreme that they name: `neighbours`: entry 0 of row l is l; every entry lies within 16 of l; for l > 0 a multiple of 16, entry 1 is l - 16.
All inputs are finite; a program needn't handle non-finite values. No bound on the sum of `cone_used` on one device may be relied on, other than what follows from the above.
Results may differ from the reference program's by a relative error of at most 0.015.
Values may be sent and summed in bfloat16 or wider, within the bound.
No kernel may reach another device: no remote copies, remote signals or barrier semaphores. Data moves between devices by JAX's collectives and lax.ppermute only.
A program may use at most 256 MiB of HBM per device.

```python
import jax
import jax.numpy as jnp
from jax import lax

K = 64
P_SIZE = 256
NB = 4
R = 128
LEAF_DEV = 16
NCL = 256
CONES = 32
LEAVES = 2048


def draw_neighbours(key, part):
    key = jax.random.fold_in(key, 7)
    key_low, key_high, key_middle = jax.random.split(key, 3)
    leaf_ids = jnp.arange(LEAVES, dtype=jnp.int32)
    lower = jax.random.randint(key_low, (LEAVES,), 1, LEAF_DEV + 1, dtype=jnp.int32)
    lower = jnp.where(leaf_ids % LEAF_DEV == 0, LEAF_DEV, lower)
    higher = jax.random.randint(key_high, (LEAVES,), 1, LEAF_DEV + 1, dtype=jnp.int32)
    middle = jax.random.randint(key_middle, (LEAVES,), -LEAF_DEV, LEAF_DEV + 1, dtype=jnp.int32)
    columns = jnp.stack([leaf_ids, leaf_ids - lower, leaf_ids + higher, leaf_ids + middle], axis=1)
    return jnp.clip(columns, 0, LEAVES - 1).astype(jnp.int32)


def touch_ends(drawn, stream_key, least, largest):
    place = [jax.random.randint(jax.random.fold_in(stream_key, axis), (), 0, length) for axis, length in enumerate(drawn.shape)]
    widest = drawn.shape.index(max(drawn.shape))
    neighbour = place[:widest] + [(place[widest] + 1) % drawn.shape[widest]] + place[widest + 1:]
    return drawn.at[tuple(place)].set(least).at[tuple(neighbour)].set(largest)


def shard_levels(rng, extent, shards, smallest, largest):
    level, own = 1.0, jax.random.fold_in(rng, 6)
    for position, shards_of in shards:
        draws = jnp.exp(jax.random.uniform(jax.random.fold_in(own, position), (shards_of,), jnp.float32, smallest / len(shards), largest / len(shards)))
        level = level * jnp.repeat(draws, extent[position] // shards_of).reshape([-1 if axis == position else 1 for axis in range(len(extent))])
    return level


def centred(own_key, extent, scale, reach, cuts=(), kind=jnp.bfloat16):
    level = shard_levels(own_key, extent, cuts, -0.22, 0.18) if cuts else 1.0
    result = jax.random.normal(own_key, extent, jnp.float32) * scale * level
    return jnp.minimum(jnp.maximum(result, -reach), reach).astype(kind)


def setup_inputs(seed: int = 0) -> dict:
    key_of = jax.random.split(jax.random.key(seed), 10)
    return {
        "upper_coef": centred(key_of[0], (NCL, CONES, 2 * K, R), 1.0, 6.0, ((0, 8), (1, 16))),
        "phase": jnp.clip(jax.random.uniform(key_of[1], (NCL, CONES, 8), jnp.float32, -3.140625, 3.140625), -3.140625, 3.140625),
        "cone_used": touch_ends((jax.random.randint(key_of[2], (NCL, CONES), 0, 4) < 3).astype(jnp.int32), jax.random.fold_in(key_of[2], 1), 0, 1),
        "transfer": centred(key_of[3], (CONES, 8, 2 * K, 2 * K), (2 * K) ** -0.5, 0.5, ((0, 16),)),
        "leaf_basis": centred(key_of[4], (LEAVES, 2, P_SIZE, 2 * K), (2 * K * CONES) ** -0.5, 0.09375, ((0, 128),)),
        "charges": centred(key_of[5], (LEAVES, P_SIZE, 2 * R), 1.0, 6.0, ((0, 128),)),
        "neighbours": draw_neighbours(jax.random.fold_in(key_of[9], 71), 0),
        "near_real": centred(key_of[7], (LEAVES, NB, P_SIZE, P_SIZE), (P_SIZE * NB) ** -0.5, 0.1875, ((0, 128),)),
        "near_imag": centred(key_of[8], (LEAVES, NB, P_SIZE, P_SIZE), (P_SIZE * NB) ** -0.5, 0.1875, ((0, 128),)),
    }


def rotate(coef, phase, cone_used):
    half = coef.shape[-2] // 2
    coef_wide = coef.astype(jnp.float32)[..., None, :, :]
    real_rows = coef_wide[..., :half, :]
    imag_rows = coef_wide[..., half:, :]
    cosines = jnp.cos(phase)[..., None, None]
    sine_part = jnp.sin(phase)[..., None, None]
    weight = cone_used.astype(jnp.float32)[..., None, None, None]
    turned = jnp.concatenate([cosines * real_rows - sine_part * imag_rows, sine_part * real_rows + cosines * imag_rows], axis=-2)
    return (turned * weight).astype(jnp.bfloat16)


def reference(upper_coef, phase, cone_used, transfer, leaf_basis, charges, neighbours, near_real, near_imag):
    transfer_wide = transfer.astype(jnp.float32)

    def one_parent(items):
        coef_p, phase_p, used_p = items
        turned = rotate(coef_p, phase_p, used_p).astype(jnp.float32)
        return jnp.einsum('coij,cojr->oir', transfer_wide, turned)

    children = lax.map(one_parent, (upper_coef, phase, cone_used))
    width = children.shape[-2]
    columns = children.shape[-1]
    leaf_round = children.reshape(LEAVES, width, columns).astype(jnp.bfloat16)
    far = jnp.einsum('lspk,lkr->lpsr', leaf_basis.astype(jnp.float32), leaf_round.astype(jnp.float32))
    far = far.reshape(LEAVES, P_SIZE, 2 * columns)
    blocks = LEAVES // LEAF_DEV

    def near_block(items):
        nbr_block, real_block, imag_block = items
        sources = charges[nbr_block].astype(jnp.float32)
        first = jnp.einsum('lnij,lnjr->lir', real_block.astype(jnp.float32), sources)
        second = jnp.einsum('lnij,lnjr->lir', imag_block.astype(jnp.float32), sources)
        return jnp.concatenate([first[..., :columns] - second[..., columns:], first[..., columns:] + second[..., :columns]], axis=-1)

    near = lax.map(near_block, (neighbours.reshape(blocks, LEAF_DEV, NB), near_real.reshape(blocks, LEAF_DEV, NB, P_SIZE, P_SIZE), near_imag.reshape(blocks, LEAF_DEV, NB, P_SIZE, P_SIZE)))
    near = near.reshape(LEAVES, P_SIZE, 2 * columns)
    return (far + near).astype(jnp.bfloat16)
```

```python
import functools

import jax
import jax.numpy as jnp
from jax import lax
from jax.experimental import pallas as pl
from jax.experimental.pallas import tpu as pltpu
from jax.sharding import PartitionSpec as P

AXES = ("cluster", "cone")
DEVICES = 128
ROW = 8
F32 = jnp.float32
BF16 = jnp.bfloat16


def moved(dx):
    return [(d, (d & ~6) | ((((d >> 1) & 3) + dx) % 4) << 1) for d in range(DEVICES)]


FLIP_CORE = [(d, d ^ 1) for d in range(DEVICES)]
FLIP_Z = [(d, d ^ 8) for d in range(DEVICES)]
FLIP_BOTH = [(d, d ^ 9) for d in range(DEVICES)]
FLIP_OUTER = [(d, d ^ 72) for d in range(DEVICES)]
X_UP = moved(1)
X_DOWN = moved(-1)
UP = [(d, d + 1) for d in range(DEVICES) if d % ROW != ROW - 1]
DOWN = [(d, d - 1) for d in range(DEVICES) if d % ROW != 0]
WRAP = [(d, d ^ 7) for d in range(DEVICES) if d % ROW in (0, ROW - 1)]
NEXT_ROW = [(d, d + ROW) for d in range(0, DEVICES - ROW, ROW)] + [
    (d, d - ROW) for d in range(2 * ROW - 1, DEVICES, ROW)
]


def permute(array, pairs):
    return lax.ppermute(array, AXES, pairs)


def split_kernel(place, coef, to_core, to_z, to_both, sems):
    zl, core = place[0], place[1]
    copies = [
        pltpu.make_async_copy(coef.at[1 - zl, :, core], to_z, sems.at[0]),
        pltpu.make_async_copy(coef.at[1 - zl, :, 1 - core], to_both, sems.at[1]),
        pltpu.make_async_copy(coef.at[zl, :, 1 - core], to_core, sems.at[2]),
    ]
    for copy in copies:
        copy.start()
    for copy in copies:
        copy.wait()


def split_coef(place, coef):
    part = jax.ShapeDtypeStruct(coef.shape[1:2] + coef.shape[3:], coef.dtype)
    return pl.pallas_call(
        split_kernel,
        out_shape=(part, part, part),
        in_specs=[pl.BlockSpec(memory_space=pltpu.SMEM), pl.BlockSpec(memory_space=pl.ANY)],
        out_specs=(pl.BlockSpec(memory_space=pl.ANY),) * 3,
        scratch_shapes=[pltpu.SemaphoreType.DMA((3,))],
        name="split_coef",
    )(place, coef)


def transfer_kernel(octants, place, targets, cosines, sines, own, c1, c2, c3, t0, t1, t2, t3, out):
    target = targets[pl.program_id(0)]
    first = pl.program_id(1) * octants
    coefs = (own.at[0, 0, 0], c1.at[0], c2.at[0], c3.at[0])
    moves = (t0, t1, t2, t3)
    half = out.shape[-2] // 2
    for o in range(octants):
        total = None
        for source in range(4):
            columns = []
            for j in range(2):
                rows = []
                for cone in range(2):
                    at = ((target * 2 + j) * 8 + source * 2 + cone) * 8 + first + o
                    cosine, sine = cosines[at], sines[at]
                    real = coefs[source][j, cone, :half, :].astype(F32)
                    imag = coefs[source][j, cone, half:, :].astype(F32)
                    rows.append((cosine * real - sine * imag).astype(BF16))
                    rows.append((sine * real + cosine * imag).astype(BF16))
                columns.append(jnp.concatenate(rows, axis=0))
            turned = jnp.concatenate(columns, axis=1)
            matrix = jnp.concatenate([moves[source][0, o], moves[source][1, o]], axis=1)
            term = jnp.dot(matrix, turned, preferred_element_type=F32)
            total = term if total is None else total + term
        width = out.shape[-1]
        out[0, 0, o] = total[:, :width].astype(BF16)
        out[0, 1, o] = total[:, width:].astype(BF16)


def transfer_terms(place, targets, cosines, sines, coefs, moves):
    count = targets.shape[0]
    octants = 4
    part = (1,) + coefs[1].shape[1:]
    matrices = (2, octants) + moves[0].shape[2:]
    own_spec = pl.BlockSpec(
        (1, 1, 1) + part[1:], lambda t, o, place, targets, *_: (place[0], targets[t], place[1], 0, 0, 0, 0)
    )
    coef_spec = pl.BlockSpec(part, lambda t, o, place, targets, *_: (targets[t], 0, 0, 0, 0))
    move_spec = pl.BlockSpec(matrices, lambda t, o, *_: (0, o, 0, 0))
    shape = (count, 2, 8) + coefs[1].shape[-2:]
    return pl.pallas_call(
        functools.partial(transfer_kernel, octants),
        out_shape=jax.ShapeDtypeStruct(shape, BF16),
        grid_spec=pltpu.PrefetchScalarGridSpec(
            num_scalar_prefetch=4,
            grid=(count, 8 // octants),
            in_specs=[own_spec] + [coef_spec] * 3 + [move_spec] * 4,
            out_specs=pl.BlockSpec((1, 2, octants) + shape[3:], lambda t, o, *_: (t, 0, o, 0, 0)),
        ),
        compiler_params=pltpu.CompilerParams(vmem_limit_bytes=32 << 20),
        cost_estimate=pl.CostEstimate(
            flops=count * 2 * 8 * 2 * 1024 * 128 * 128, bytes_accessed=(count + 3) << 20, transcendentals=0
        ),
        name="transfer_terms",
    )(place, targets, cosines, sines, *coefs, *moves)


def apply_kernel(ids, edge, near_real, near_imag, basis, leaf0, leaf1, leaf2, below, own, above, wrapped, out, sources, sems):
    leaf = pl.program_id(0)
    count = own.shape[0]
    columns = leaf0.shape[-1]
    low, middle, high = (sources.at[pl.ds(i * count, count)] for i in range(3))

    @pl.when(leaf == 0)
    def _():
        copy_own = pltpu.make_async_copy(own, middle, sems.at[0])
        copy_own.start()

        @pl.when(edge[0] == 1)
        def _():
            pltpu.make_async_copy(wrapped, low, sems.at[1]).start()

        @pl.when(edge[0] == 0)
        def _():
            pltpu.make_async_copy(below, low, sems.at[1]).start()

        @pl.when(edge[1] == 1)
        def _():
            pltpu.make_async_copy(wrapped, high, sems.at[2]).start()

        @pl.when(edge[1] == 0)
        def _():
            pltpu.make_async_copy(above, high, sems.at[2]).start()

        copy_own.wait()
        pltpu.make_async_copy(below, low, sems.at[1]).wait()
        pltpu.make_async_copy(above, high, sems.at[2]).wait()

    coef = (leaf0[0].astype(F32) + leaf1[0].astype(F32) + leaf2[0].astype(F32)).astype(BF16)
    total = jnp.concatenate(
        [jnp.dot(basis[0, s], coef, preferred_element_type=F32) for s in range(2)], axis=1
    )
    for n in range(4):
        charge = sources[ids[leaf * 4 + n]]
        crossed = jnp.concatenate([-charge[:, columns:], charge[:, :columns]], axis=1)
        total += jnp.dot(near_real[0, n], charge, preferred_element_type=F32)
        total += jnp.dot(near_imag[0, n], crossed, preferred_element_type=F32)
    out[0] = total.astype(BF16)


def apply_leaves(ids, edge, near_real, near_imag, basis, leaf_terms, below, own, above, wrapped):
    count, points, wide = own.shape
    matrices = pl.BlockSpec((1,) + near_real.shape[1:], lambda l, *_: (l, 0, 0, 0))
    leaf_spec = pl.BlockSpec((1,) + leaf_terms[0].shape[1:], lambda l, *_: (l, 0, 0))
    anywhere = pl.BlockSpec(memory_space=pl.ANY)
    return pl.pallas_call(
        apply_kernel,
        out_shape=jax.ShapeDtypeStruct(own.shape, BF16),
        grid_spec=pltpu.PrefetchScalarGridSpec(
            num_scalar_prefetch=2,
            grid=(count,),
            in_specs=[matrices, matrices, pl.BlockSpec((1,) + basis.shape[1:], lambda l, *_: (l, 0, 0, 0))]
            + [leaf_spec] * 3
            + [anywhere] * 4,
            out_specs=pl.BlockSpec((1, points, wide), lambda l, *_: (l, 0, 0)),
            scratch_shapes=[pltpu.VMEM((3 * count, points, wide), BF16), pltpu.SemaphoreType.DMA((3,))],
        ),
        compiler_params=pltpu.CompilerParams(vmem_limit_bytes=32 << 20),
        cost_estimate=pl.CostEstimate(flops=4_600_000_000, bytes_accessed=28 << 20, transcendentals=0),
        name="apply_leaves",
    )(ids, edge, near_real, near_imag, basis, *leaf_terms, below, own, above, wrapped)


def per_device(
    upper_coef, phase, cone_used, transfer, leaf_basis, charges, neighbours, near_real, near_imag
):
    leaf_count = charges.shape[0]
    cluster, cone = lax.axis_index("cluster"), lax.axis_index("cone")
    zl, x, core = cone // 8, (cone // 2) % 4, cone % 2
    place = jnp.stack([zl, core]).astype(jnp.int32)

    coef = upper_coef.reshape((2, 4, 2, 2) + upper_coef.shape[1:])
    to_core, to_z, to_both = split_coef(place, coef)
    from_z = permute(to_z, FLIP_Z)
    from_both = permute(to_both, FLIP_BOTH)
    from_core = permute(to_core, FLIP_CORE)

    below = permute(charges, UP)
    above = permute(charges, DOWN)
    wrapped = permute(permute(charges, WRAP), NEXT_ROW)

    weight = cone_used.astype(F32)[..., None]
    turn = jnp.stack([jnp.cos(phase) * weight, jnp.sin(phase) * weight])
    turn = turn.reshape((2, 2, 4, 2, 2) + turn.shape[2:])

    def turn_of(z, c):
        return turn[:, z, :, c]

    turns = [
        turn_of(zl, core),
        permute(turn_of(zl, 1 - core), FLIP_CORE),
        permute(turn_of(1 - zl, core), FLIP_Z),
        permute(turn_of(1 - zl, 1 - core), FLIP_BOTH),
    ]
    turns = jnp.stack(turns, axis=3)
    cosines, sines = turns[0].reshape(-1), turns[1].reshape(-1)

    transfer_outer = permute(transfer, FLIP_OUTER)
    moves = [transfer, permute(transfer, FLIP_CORE), transfer_outer, permute(transfer_outer, FLIP_CORE)]
    coefs = [coef, from_core, from_z, from_both]

    def terms(offsets):
        targets = jnp.stack([(x + offset) % 4 for offset in offsets]).astype(jnp.int32)
        return transfer_terms(place, targets, cosines, sines, coefs, moves)

    far_terms = terms([2])
    up = permute(far_terms[0, 0], X_UP)
    down = permute(far_terms[0, 1], X_DOWN)
    rest = terms([1, 3, 0])

    def added(a, b):
        return (a.astype(F32) + b.astype(F32)).astype(BF16)

    from_below = permute(jnp.stack([added(rest[0, 0], up), rest[0, 1]]), X_UP)
    from_above = permute(jnp.stack([rest[1, 0], added(rest[1, 1], down)]), X_DOWN)
    leaf_terms = [
        part.reshape((leaf_count,) + part.shape[-2:]) for part in (rest[2], from_below, from_above)
    ]

    first_leaf = (cluster * 16 + cone) * leaf_count
    ids = (neighbours - first_leaf + leaf_count).reshape(-1)
    edge = jnp.stack([cone % ROW == 0, cone % ROW == ROW - 1]).astype(jnp.int32)
    return apply_leaves(
        ids, edge, near_real, near_imag, leaf_basis, leaf_terms, below, charges, above, wrapped
    )


def solution(mesh):
    in_specs = (
        P("cluster", "cone", None, None),
        P("cluster", "cone", None),
        P("cluster", "cone"),
        P("cone", None, None, None),
        P(("cluster", "cone"), None, None, None),
        P(("cluster", "cone"), None, None),
        P(("cluster", "cone"), None),
        P(("cluster", "cone"), None, None, None),
        P(("cluster", "cone"), None, None, None),
    )
    out_specs = P(("cluster", "cone"), None, None)
    return jax.shard_map(
        per_device, mesh=mesh, in_specs=in_specs, out_specs=out_specs, check_vma=False
    )
```

```python
import jax
import jax.numpy as jnp
from jax import lax
from jax.experimental import pallas as pl
from jax.experimental.pallas import tpu as pltpu
from jax.sharding import PartitionSpec as P

AXES = ("cluster", "cone")
DEVICES = 128
ROW = 8
F32 = jnp.float32
BF16 = jnp.bfloat16
SMALL = pl.CostEstimate(flops=0, bytes_accessed=1024, transcendentals=0)


def moved(dx):
    return [(d, (d & ~6) | ((((d >> 1) & 3) + dx) % 4) << 1) for d in range(DEVICES)]


FLIP_CORE = [(d, d ^ 1) for d in range(DEVICES)]
FLIP_Z = [(d, d ^ 8) for d in range(DEVICES)]
FLIP_BOTH = [(d, d ^ 9) for d in range(DEVICES)]
FLIP_OUTER = [(d, d ^ 72) for d in range(DEVICES)]
X_UP = moved(1)
X_DOWN = moved(-1)
UP = [(d, d + 1) for d in range(DEVICES) if d % ROW != ROW - 1]
DOWN = [(d, d - 1) for d in range(DEVICES) if d % ROW != 0]
WRAP = [(d, d ^ 7) for d in range(DEVICES) if d % ROW in (0, ROW - 1)]
NEXT_ROW = [(d, d + ROW) for d in range(0, DEVICES - ROW, ROW)] + [
    (d, d - ROW) for d in range(2 * ROW - 1, DEVICES, ROW)
]


def permute(array, pairs):
    return lax.ppermute(array, AXES, pairs)


IN_VMEM = pl.BlockSpec(memory_space=pltpu.VMEM)
IN_HBM = pl.BlockSpec(memory_space=pltpu.HBM)
IN_SMEM = pl.BlockSpec(memory_space=pltpu.SMEM)
ANYWHERE = pl.BlockSpec(memory_space=pl.ANY)


def kept_in_hbm(array):
    return pltpu.with_memory_space_constraint(array, pltpu.HBM)


def kept_in_vmem(array):
    return pltpu.with_memory_space_constraint(array, pltpu.VMEM)


def limit(mib):
    return pltpu.CompilerParams(vmem_limit_bytes=mib << 20)


def stage_kernel(coef, charges, *refs):
    outs, buffers, sems = refs[:5], refs[5:10], refs[10]
    cone = lax.axis_index("cone")
    zl, core = cone // 8, cone % 2
    sources = (
        coef.at[1 - zl, :, core],
        coef.at[1 - zl, :, 1 - core],
        coef.at[zl, :, 1 - core],
        coef.at[zl, :, core],
        charges,
    )
    loads = [pltpu.make_async_copy(sources[i], buffers[i], sems.at[0, i]) for i in range(5)]
    stores = [pltpu.make_async_copy(buffers[i], outs[i], sems.at[1, i]) for i in range(5)]
    for load in loads:
        load.start()
    for load, store in zip(loads, stores):
        load.wait()
        store.start()
    for store in stores:
        store.wait()


def stage(coef, charges):
    part = jax.ShapeDtypeStruct(coef.shape[1:2] + coef.shape[3:], coef.dtype)
    outs = (part,) * 4 + (jax.ShapeDtypeStruct(charges.shape, charges.dtype),)
    return pl.pallas_call(
        stage_kernel,
        out_shape=outs,
        in_specs=[IN_HBM, IN_HBM],
        out_specs=(IN_HBM,) * 5,
        scratch_shapes=[pltpu.VMEM(out.shape, out.dtype) for out in outs] + [pltpu.SemaphoreType.DMA((2, 5))],
        compiler_params=limit(6),
        cost_estimate=SMALL,
        name="stage",
    )(kept_in_hbm(coef), kept_in_hbm(charges))


def tied(array, *others):
    def kernel(*refs):
        del refs

    return pl.pallas_call(
        kernel,
        out_shape=jax.ShapeDtypeStruct(array.shape, array.dtype),
        in_specs=[ANYWHERE] * (1 + len(others)),
        out_specs=ANYWHERE,
        input_output_aliases={0: 0},
        cost_estimate=SMALL,
        name="tied",
    )(array, *others)


def transfer_kernel(count, ties, targets, cosines, sines, *refs):
    coefs, moves = refs[:4], refs[4:8]
    outs = refs[8 + ties : 8 + ties + 2 * count]
    coef_in, move_in, coef_sems, move_sems = refs[8 + ties + 2 * count :]
    width = outs[0].shape[-1]
    half = outs[0].shape[-2] // 2

    def coef_load(t, source):
        return pltpu.make_async_copy(coefs[source].at[targets[t]], coef_in.at[t, source], coef_sems.at[t, source])

    def move_load(part, source):
        octants = pl.ds(0, 2) if part == 0 else pl.ds(2, 6)
        return pltpu.make_async_copy(
            moves[source].at[:, octants], move_in.at[source, :, octants], move_sems.at[part, source]
        )

    for part in range(2):
        for source in range(4):
            if part < count:
                coef_load(part, source).start()
            move_load(part, source).start()
    for t in range(2, count):
        for source in range(4):
            coef_load(t, source).start()

    for t in range(count):
        for source in range(4):
            coef_load(t, source).wait()
        for o in range(8):
            if t == 0 and o in (0, 2):
                for source in range(4):
                    move_load(o // 2, source).wait()
            total = None
            for source in range(4):
                columns = []
                for j in range(2):
                    rows = []
                    for cone in range(2):
                        at = ((targets[t] * 2 + j) * 8 + source * 2 + cone) * 8 + o
                        cosine, sine = cosines[at], sines[at]
                        real = coef_in[t, source, j, cone, :half, :].astype(F32)
                        imag = coef_in[t, source, j, cone, half:, :].astype(F32)
                        rows.append((cosine * real - sine * imag).astype(BF16))
                        rows.append((sine * real + cosine * imag).astype(BF16))
                    columns.append(jnp.concatenate(rows, axis=0))
                turned = jnp.concatenate(columns, axis=1)
                matrix = jnp.concatenate([move_in[source, 0, o], move_in[source, 1, o]], axis=1)
                term = jnp.dot(matrix, turned, preferred_element_type=F32)
                total = term if total is None else total + term
            for j in range(2):
                outs[t * 2 + j][o] = total[:, j * width : (j + 1) * width].astype(BF16)


def transfer_terms(targets, cosines, sines, coefs, moves, ties=()):
    count = targets.shape[0]
    out = pltpu.VMEM((8,) + coefs[0].shape[-2:], BF16)

    def kernel(*refs):
        transfer_kernel(count, len(ties), *refs)

    return pl.pallas_call(
        kernel,
        out_shape=(out,) * (2 * count),
        in_specs=[IN_SMEM] * 3 + [IN_HBM] * 8 + [ANYWHERE] * len(ties),
        out_specs=(IN_VMEM,) * (2 * count),
        scratch_shapes=[
            pltpu.VMEM((count, 4) + coefs[0].shape[1:], BF16),
            pltpu.VMEM((4,) + moves[0].shape, BF16),
            pltpu.SemaphoreType.DMA((count, 4)),
            pltpu.SemaphoreType.DMA((2, 4)),
        ],
        compiler_params=limit(8),
        cost_estimate=SMALL,
        name="transfer_terms",
    )(targets, cosines, sines, *[kept_in_hbm(a) for a in coefs], *[kept_in_hbm(a) for a in moves], *ties)


def add_kernel(left, right, arrived, out):
    for o in range(8):
        out[0, o] = left[o]
        out[1, o] = (right[o].astype(F32) + arrived[o].astype(F32)).astype(BF16)


def with_arrived(left, right, arrived):
    return pl.pallas_call(
        add_kernel,
        out_shape=pltpu.VMEM((2,) + left.shape, BF16),
        in_specs=[IN_VMEM] * 3,
        out_specs=IN_VMEM,
        compiler_params=limit(2),
        cost_estimate=SMALL,
        name="with_arrived",
    )(left, right, kept_in_vmem(arrived))


def pair_term(real, imag, charge):
    points, columns = charge.shape[0], charge.shape[1] // 2
    both = jnp.dot(jnp.concatenate([real, imag], axis=0), charge, preferred_element_type=F32)
    first, second = both[:points], both[points:]
    return jnp.concatenate(
        [first[:, :columns] - second[:, columns:], first[:, columns:] + second[:, :columns]], axis=1
    )


GROUP = 4
AHEAD = 3
PAIRS = 64


SLOTS = (AHEAD + 1) * GROUP


def pair_scratch(points, wide):
    block = pltpu.VMEM((SLOTS, points, wide), BF16)
    return [block, block, block, pltpu.SemaphoreType.DMA((3, SLOTS))]


def listed_pairs(listed, ids, near_real, near_imag, charges_of, sums, reals, imags, charges, sems):
    length = listed[0]
    groups = (length + GROUP - 1) // GROUP

    def blocks(place):
        pair = listed[1 + place]
        leaf, n = pair // 4, pair % 4
        slot = lax.rem(place, SLOTS)
        return (
            pltpu.make_async_copy(near_real.at[leaf, n], reals.at[slot], sems.at[0, slot]),
            pltpu.make_async_copy(near_imag.at[leaf, n], imags.at[slot], sems.at[1, slot]),
        )

    def charge_load(source, place):
        slot = lax.rem(place, SLOTS)
        return pltpu.make_async_copy(source, charges.at[slot], sems.at[2, slot])

    def start(place):
        @pl.when(place < length)
        def _():
            for copy in blocks(place):
                copy.start()
            for case, source in charges_of(ids[listed[1 + place]]):

                @pl.when(case)
                def _():
                    charge_load(source, place).start()

    def finish(place):
        @pl.when(place < length)
        def _():
            for copy in blocks(place):
                copy.wait()
            _, source = charges_of(ids[listed[1 + place]])[0]
            charge_load(source, place).wait()

    for place in range(AHEAD * GROUP):
        start(place)

    @pl.loop(0, groups)
    def _(group):
        for i in range(GROUP):
            start((group + AHEAD) * GROUP + i)
        for i in range(GROUP):
            finish(group * GROUP + i)
        terms = []
        for i in range(GROUP):
            place = group * GROUP + i
            inside = place < length
            place = jnp.where(inside, place, length - 1)
            slot = lax.rem(place, SLOTS)
            charge = charges[slot]
            charge = jnp.where(inside, charge, jnp.zeros_like(charge))
            terms.append((listed[1 + place] // 4, pair_term(reals[slot], imags[slot], charge)))
        for leaf, term in terms:
            sums[leaf] += term


def own_kernel(ids, near_real, near_imag, basis, own, bases, sums, beside, wrapping, inner, basis_sem, *scratch):
    count = own.shape[0]
    load_basis = pltpu.make_async_copy(basis, bases, basis_sem)
    load_basis.start()
    at_row = lax.rem(lax.axis_index("cone"), ROW)

    for listed in (inner, beside, wrapping):
        listed[0] = 0

    @pl.loop(0, count * 4)
    def _(pair):
        at = ids[pair]
        low, high = at < count, at >= 2 * count
        wraps = (low & (at_row == 0)) | (high & (at_row == ROW - 1))

        def put(listed):
            length = listed[0] + 1
            listed[0] = length
            listed[length] = pair

        @pl.when(jnp.logical_not(low | high))
        def _():
            put(inner)

        @pl.when(wraps)
        def _():
            put(wrapping)

        @pl.when((low | high) & jnp.logical_not(wraps))
        def _():
            put(beside)

    @pl.loop(0, count)
    def _(leaf):
        sums[leaf] = jnp.zeros(sums.shape[1:], F32)

    def charges_of(at):
        return [(True, own.at[at - count])]

    listed_pairs(inner, ids, near_real, near_imag, charges_of, sums, *scratch)
    load_basis.wait()


def own_sums(ids, near_real, near_imag, basis, own):
    pairs = jax.ShapeDtypeStruct((1 + PAIRS,), jnp.int32)
    return pl.pallas_call(
        own_kernel,
        out_shape=(pltpu.VMEM(basis.shape, BF16), pltpu.VMEM(own.shape, F32), pairs, pairs),
        in_specs=[IN_SMEM] + [IN_HBM] * 4,
        out_specs=(IN_VMEM,) * 2 + (IN_SMEM,) * 2,
        scratch_shapes=[pltpu.SMEM(pairs.shape, jnp.int32), pltpu.SemaphoreType.DMA]
        + pair_scratch(*own.shape[1:]),
        compiler_params=limit(9),
        cost_estimate=SMALL,
        name="own_sums",
    )(ids, kept_in_hbm(near_real), kept_in_hbm(near_imag), kept_in_hbm(basis), kept_in_hbm(own))


def beside_kernel(ids, listed, near_real, near_imag, below, above, before, sums, *scratch):
    count = below.shape[0]
    del before

    def charges_of(at):
        inside = lax.rem(at, count)
        return [(at < count, below.at[inside]), (at >= count, above.at[inside])]

    listed_pairs(listed, ids, near_real, near_imag, charges_of, sums, *scratch)


def beside_sums(ids, listed, near_real, near_imag, below, above, sums):
    return pl.pallas_call(
        beside_kernel,
        out_shape=pltpu.VMEM(sums.shape, F32),
        in_specs=[IN_SMEM] * 2 + [IN_HBM] * 4 + [IN_VMEM],
        out_specs=IN_VMEM,
        input_output_aliases={6: 0},
        scratch_shapes=pair_scratch(*sums.shape[1:]),
        compiler_params=limit(9),
        cost_estimate=SMALL,
        name="beside_sums",
    )(ids, listed, kept_in_hbm(near_real), kept_in_hbm(near_imag), kept_in_hbm(below), kept_in_hbm(above), sums)


def apply_kernel(
    ids, listed, near_real, near_imag, wrapped, before, basis, leaf00, leaf01, leaf1, leaf2, out, sums, totals, store_sems, *scratch
):
    count = wrapped.shape[0]
    del before

    def charges_of(at):
        return [(True, wrapped.at[lax.rem(at, count)])]

    def store(leaf):
        return pltpu.make_async_copy(totals.at[leaf], out.at[leaf], store_sems.at[leaf])

    listed_pairs(listed, ids, near_real, near_imag, charges_of, sums, *scratch)
    for j, own in enumerate((leaf00, leaf01)):

        @pl.loop(0, count // 4)
        def _(half):
            for i in range(2):
                o = 2 * half + i
                leaf = j * (count // 2) + o
                coef = own[o].astype(F32) + leaf1[1 - j, o].astype(F32) + leaf2[j, o].astype(F32)
                coef = coef.astype(BF16)
                far = [jnp.dot(basis[leaf, s], coef, preferred_element_type=F32) for s in range(2)]
                totals[leaf] = (sums[leaf] + jnp.concatenate(far, axis=1)).astype(BF16)
                store(leaf).start()

    for leaf in range(count):
        store(leaf).wait()


def apply_leaves(ids, listed, near_real, near_imag, wrapped, sums, basis, leaf_terms):
    count = sums.shape[0]
    leaf_terms = leaf_terms[:2] + [kept_in_vmem(a) for a in leaf_terms[2:]]
    return pl.pallas_call(
        apply_kernel,
        out_shape=(jax.ShapeDtypeStruct(sums.shape, BF16), pltpu.VMEM(sums.shape, F32)),
        in_specs=[IN_SMEM] * 2 + [IN_HBM] * 3 + [IN_VMEM] * 6,
        out_specs=(IN_HBM, IN_VMEM),
        input_output_aliases={5: 1},
        scratch_shapes=[pltpu.VMEM(sums.shape, BF16), pltpu.SemaphoreType.DMA((count,))]
        + pair_scratch(*sums.shape[1:]),
        compiler_params=limit(11),
        cost_estimate=SMALL,
        name="apply_leaves",
    )(ids, listed, kept_in_hbm(near_real), kept_in_hbm(near_imag), kept_in_hbm(wrapped), sums, basis, *leaf_terms)[0]


def per_device(
    upper_coef, phase, cone_used, transfer, leaf_basis, charges, neighbours, near_real, near_imag
):
    leaf_count = charges.shape[0]
    cluster, cone = lax.axis_index("cluster"), lax.axis_index("cone")
    zl, x, core = cone // 8, (cone // 2) % 4, cone % 2

    coef = upper_coef.reshape((2, 4, 2, 2) + upper_coef.shape[1:])
    to_z, to_both, to_core, kept, staged = stage(coef, charges)
    from_z = permute(to_z, FLIP_Z)
    from_both = permute(to_both, FLIP_BOTH)
    from_core = permute(to_core, FLIP_CORE)

    weight = cone_used.astype(F32)[..., None]
    turn = jnp.stack([jnp.cos(phase) * weight, jnp.sin(phase) * weight])
    turn = turn.reshape((2, 2, 4, 2, 2) + turn.shape[2:])

    def turn_of(z, c):
        return turn[:, z, :, c]

    turns = [
        turn_of(zl, core),
        permute(turn_of(zl, 1 - core), FLIP_CORE),
        permute(turn_of(1 - zl, core), FLIP_Z),
        permute(turn_of(1 - zl, 1 - core), FLIP_BOTH),
    ]
    staged = tied(staged, *turns[1:])
    turns = jnp.stack(turns, axis=3)
    cosines, sines = turns[0].reshape(-1), turns[1].reshape(-1)

    transfer_outer = permute(transfer, FLIP_OUTER)
    moves = [transfer, permute(transfer, FLIP_CORE), transfer_outer, permute(transfer_outer, FLIP_CORE)]
    coefs = [kept, from_core, from_z, from_both]

    first_leaf = (cluster * 16 + cone) * leaf_count
    ids = (neighbours - first_leaf + leaf_count).reshape(-1)
    basis, sums, beside, wrapping = own_sums(ids, near_real, near_imag, leaf_basis, staged)

    below = permute(staged, UP)
    above = permute(staged, DOWN)
    crossed = tied(permute(staged, WRAP), from_z, from_both, transfer_outer, beside)
    wrapped = permute(crossed, NEXT_ROW)

    def terms(offsets, ties=()):
        targets = jnp.stack([(x + offset) % 4 for offset in offsets]).astype(jnp.int32)
        return transfer_terms(targets, cosines, sines, coefs, moves, ties)

    far_first, far_second = terms([2], [beside])
    up = permute(far_first, X_UP)
    down = permute(far_second, X_DOWN)
    up_first, up_second, down_first, down_second, own_first, own_second = terms([1, 3, 0], [below, above])
    from_below = permute(with_arrived(up_second, up_first, up), X_UP)
    from_above = permute(with_arrived(down_first, down_second, down), X_DOWN)
    sums = beside_sums(ids, beside, near_real, near_imag, below, above, sums)
    leaf_terms = [own_first, own_second, from_below, from_above]
    return apply_leaves(ids, wrapping, near_real, near_imag, wrapped, sums, basis, leaf_terms)


def solution(mesh):
    in_specs = (
        P("cluster", "cone", None, None),
        P("cluster", "cone", None),
        P("cluster", "cone"),
        P("cone", None, None, None),
        P(("cluster", "cone"), None, None, None),
        P(("cluster", "cone"), None, None),
        P(("cluster", "cone"), None),
        P(("cluster", "cone"), None, None, None),
        P(("cluster", "cone"), None, None, None),
    )
    out_specs = P(("cluster", "cone"), None, None)
    return jax.shard_map(
        per_device, mesh=mesh, in_specs=in_specs, out_specs=out_specs, check_vma=False
    )
```

```python
import jax
import jax.numpy as jnp
from jax import lax
from jax.experimental import pallas as pl
from jax.experimental.pallas import tpu as pltpu
from jax.sharding import PartitionSpec as P

AXES = ("cluster", "cone")
DEVICES = 128
ROW = 8
F32 = jnp.float32
BF16 = jnp.bfloat16
SMALL = pl.CostEstimate(flops=0, bytes_accessed=1024, transcendentals=0)


def moved(dx):
    return [(d, (d & ~6) | ((((d >> 1) & 3) + dx) % 4) << 1) for d in range(DEVICES)]


FLIP_CORE = [(d, d ^ 1) for d in range(DEVICES)]
FLIP_Z = [(d, d ^ 8) for d in range(DEVICES)]
FLIP_BOTH = [(d, d ^ 9) for d in range(DEVICES)]
FLIP_OUTER = [(d, d ^ 72) for d in range(DEVICES)]
X_UP = moved(1)
X_DOWN = moved(-1)
UP = [(d, d - d % ROW + (d + 1) % ROW) for d in range(DEVICES)]
DOWN = [(d, d - d % ROW + (d - 1) % ROW) for d in range(DEVICES)]
NEXT_ROW = [(d, d + ROW) for d in range(0, DEVICES - ROW, ROW)] + [
    (d, d - ROW) for d in range(2 * ROW - 1, DEVICES, ROW)
]


def permute(array, pairs):
    return lax.ppermute(array, AXES, pairs)


IN_VMEM = pl.BlockSpec(memory_space=pltpu.VMEM)
IN_HBM = pl.BlockSpec(memory_space=pltpu.HBM)
IN_SMEM = pl.BlockSpec(memory_space=pltpu.SMEM)
ANYWHERE = pl.BlockSpec(memory_space=pl.ANY)


def kept_in_hbm(array):
    return pltpu.with_memory_space_constraint(array, pltpu.HBM)


def kept_in_vmem(array):
    return pltpu.with_memory_space_constraint(array, pltpu.VMEM)


def limit(mib):
    return pltpu.CompilerParams(vmem_limit_bytes=mib << 20)


ANGLES = 16
TAIL = 4 * ANGLES


def stage_kernel(angle, used, coef, transfer, *refs):
    outs, buffers, angles, weights, sems = refs[:5], refs[5:10], refs[10], refs[11], refs[12]
    small = [pltpu.make_async_copy(angle, angles, sems.at[1, 5]), pltpu.make_async_copy(used, weights, sems.at[1, 6])]
    for copy in small:
        copy.start()
    cone = lax.axis_index("cone")
    zl, core = cone // 8, cone % 2
    sources = ((1 - zl, core), (1 - zl, 1 - core), (zl, 1 - core), (zl, core))
    rows = coef.shape[-2]
    loads = [
        [
            pltpu.make_async_copy(coef.at[z, x, c], buffers[i].at[pl.ds(x * rows, rows)], sems.at[0, i * 4 + x])
            for x in range(4)
        ]
        for i, (z, c) in enumerate(sources)
    ] + [[pltpu.make_async_copy(transfer, buffers[4], sems.at[0, 16])]]
    stores = [pltpu.make_async_copy(buffers[i], outs[i], sems.at[1, i]) for i in range(5)]
    for part in loads:
        for load in part:
            load.start()

    for copy in small:
        copy.wait()
    high = angles[...].astype(BF16)
    left = angles[...] - high.astype(F32)
    middle = left.astype(BF16)
    low = (left - middle.astype(F32)).astype(BF16)
    weight = weights[...].astype(F32)
    each = (ANGLES // 2, weight.shape[1])
    weight = jnp.concatenate([jnp.broadcast_to(weight[i : i + 1], each) for i in range(2)], axis=0)
    for buffer in buffers[:4]:
        buffer[4 * rows :, :] = jnp.zeros((TAIL, buffer.shape[1]), BF16)
        for i, piece in enumerate((high, middle, low, weight.astype(BF16))):
            start = 4 * rows + i * ANGLES
            buffer[start : start + ANGLES, : piece.shape[1]] = piece

    for part, store in zip(loads, stores):
        for load in part:
            load.wait()
        store.start()
    for store in stores:
        store.wait()


def stage(angle, used, coef, transfer):
    part = jax.ShapeDtypeStruct((4 * coef.shape[-2] + TAIL, coef.shape[-1]), coef.dtype)
    outs = (part,) * 4 + (jax.ShapeDtypeStruct(transfer.shape, transfer.dtype),)
    return pl.pallas_call(
        stage_kernel,
        out_shape=outs,
        in_specs=[IN_HBM] * 4,
        out_specs=(IN_HBM,) * 5,
        scratch_shapes=[pltpu.VMEM(a.shape, a.dtype) for a in (*outs, angle, used)]
        + [pltpu.SemaphoreType.DMA((2, 17))],
        compiler_params=limit(5),
        cost_estimate=SMALL,
        name="stage",
    )(*[kept_in_hbm(a) for a in (angle, used, coef, transfer)])


def tied(array, *others):
    def kernel(*refs):
        del refs

    return pl.pallas_call(
        kernel,
        out_shape=jax.ShapeDtypeStruct(array.shape, array.dtype),
        in_specs=[ANYWHERE] * (1 + len(others)),
        out_specs=ANYWHERE,
        input_output_aliases={0: 0},
        compiler_params=limit(1),
        cost_estimate=SMALL,
        name="tied",
    )(array, *others)


def cross_kernel(ties, below, above, *refs):
    out, buffer, sem = refs[ties:]
    at_row = lax.rem(lax.axis_index("cone"), ROW)

    def carry(source):
        for copy in (pltpu.make_async_copy(source, buffer, sem), pltpu.make_async_copy(buffer, out, sem)):
            copy.start()
            copy.wait()

    @pl.when(at_row == 0)
    def _():
        carry(below)

    @pl.when(at_row == ROW - 1)
    def _():
        carry(above)


def crossing_charges(below, above, ties):
    def kernel(*refs):
        cross_kernel(len(ties), *refs)

    return pl.pallas_call(
        kernel,
        out_shape=jax.ShapeDtypeStruct(below.shape, below.dtype),
        in_specs=[ANYWHERE] * (2 + len(ties)),
        out_specs=ANYWHERE,
        scratch_shapes=[pltpu.VMEM(below.shape, below.dtype), pltpu.SemaphoreType.DMA],
        compiler_params=limit(3),
        cost_estimate=SMALL,
        name="crossing_charges",
    )(below, above, *ties)


def transfer_kernel(offsets, ties, *refs):
    coefs, moves, outs = refs[:4], refs[4:8], refs[8 + ties :]
    cone_index = lax.axis_index("cone")
    zl, x, core = cone_index // 8, (cone_index // 2) % 4, cone_index % 2
    size, width = outs[0].shape[1:]
    half = size // 2
    lanes = lax.broadcasted_iota(jnp.int32, (ANGLES, width), 1)
    turns = []
    for coef in coefs:
        tail = coef[coef.shape[0] - TAIL :, :].astype(F32)
        high, middle, low, weight = (tail[i * ANGLES : (i + 1) * ANGLES] for i in range(4))
        angle = high + middle + low
        turns.append((jnp.cos(angle) * weight, jnp.sin(angle) * weight))

    for t, offset in enumerate(offsets):
        target = (x + offset) % 4
        first = zl * 16 + target * 4 + core * 2
        columns_of = [
            [
                [
                    jnp.sum(jnp.where(lanes == first + j, part, 0.0), axis=1, keepdims=True)
                    for part in turns[source]
                ]
                for j in range(2)
            ]
            for source in range(4)
        ]
        for o in range(8):
            total = None
            for source in range(4):
                columns = []
                for j in range(2):
                    rows = []
                    for cone in range(2):
                        at = cone * 8 + o
                        cosine, sine = (column[at : at + 1] for column in columns_of[source][j])
                        start = pl.multiple_of(((target * 2 + j) * 2 + cone) * size, size)
                        real = coefs[source][pl.ds(start, half), :].astype(F32)
                        imag = coefs[source][pl.ds(start + half, half), :].astype(F32)
                        rows.append((cosine * real - sine * imag).astype(BF16))
                        rows.append((sine * real + cosine * imag).astype(BF16))
                    columns.append(jnp.concatenate(rows, axis=0))
                turned = jnp.concatenate(columns, axis=1)
                matrix = jnp.concatenate([moves[source][0, o], moves[source][1, o]], axis=1)
                term = jnp.dot(matrix, turned, preferred_element_type=F32)
                total = term if total is None else total + term
            for j in range(2):
                outs[t * 2 + j][o] = total[:, j * width : (j + 1) * width].astype(BF16)


def transfer_terms(offsets, coefs, moves, ties=()):
    out = pltpu.VMEM(moves[0].shape[1:], BF16)

    def kernel(*refs):
        transfer_kernel(offsets, len(ties), *refs)

    return pl.pallas_call(
        kernel,
        out_shape=(out,) * (2 * len(offsets)),
        in_specs=[IN_VMEM] * 8 + [ANYWHERE] * len(ties),
        out_specs=(IN_VMEM,) * (2 * len(offsets)),
        compiler_params=limit(8),
        cost_estimate=SMALL,
        name="transfer_terms",
    )(*[kept_in_vmem(a) for a in coefs], *[kept_in_vmem(a) for a in moves], *ties)


def add_kernel(left, right, arrived, *rest):
    out = rest[-1]
    for o in range(8):
        out[0, o] = left[o]
        out[1, o] = (right[o].astype(F32) + arrived[o].astype(F32)).astype(BF16)


def with_arrived(left, right, arrived, ties=()):
    return pl.pallas_call(
        add_kernel,
        out_shape=pltpu.VMEM((2,) + left.shape, BF16),
        in_specs=[IN_VMEM] * 3 + [ANYWHERE] * len(ties),
        out_specs=IN_VMEM,
        compiler_params=limit(2),
        cost_estimate=SMALL,
        name="with_arrived",
    )(left, right, kept_in_vmem(arrived), *ties)


def pair_term(real, imag, charge):
    points, columns = charge.shape[0], charge.shape[1] // 2
    both = jnp.dot(jnp.concatenate([real, imag], axis=0), charge, preferred_element_type=F32)
    first, second = both[:points], both[points:]
    return jnp.concatenate(
        [first[:, :columns] - second[:, columns:], first[:, columns:] + second[:, :columns]], axis=1
    )


GROUP = 4
PAIRS = 64


def place_of(neighbours, pair):
    count = neighbours.shape[1]
    device = lax.axis_index("cluster") * 16 + lax.axis_index("cone")
    return neighbours[pair % 4, pair // 4] - (device - 1) * count


def listed_pairs(listed, reals, imags, charge_of, sums, ready=None):
    length = listed[0]

    @pl.loop(0, (length + GROUP - 1) // GROUP)
    def _(group):
        places = [group * GROUP + i for i in range(GROUP)]
        pairs = [listed[1 + jnp.minimum(place, length - 1)] for place in places]
        if ready is not None:
            ready(pairs[-1] // 4)
        terms = []
        for place, pair in zip(places, pairs):
            charge = charge_of(pair)
            charge = jnp.where(place < length, charge, jnp.zeros_like(charge))
            leaf, n = pair // 4, pair % 4
            terms.append((leaf, pair_term(reals[leaf, n], imags[leaf, n], charge)))
        for leaf, term in terms:
            sums[leaf] += term


LEAVES_AHEAD = 5


def own_kernel(
    ties, neighbours, near_real, near_imag, basis, own, *refs
):
    reals, imags, bases, sums, beside, wrapping, inner, charges, loaded, sems, other_sems = refs[ties:]
    count = own.shape[0]
    load_charges = pltpu.make_async_copy(own, charges, other_sems.at[0])
    load_basis = pltpu.make_async_copy(basis, bases, other_sems.at[1])

    def loads(leaf):
        return (
            pltpu.make_async_copy(near_real.at[leaf], reals.at[leaf], sems.at[0, leaf]),
            pltpu.make_async_copy(near_imag.at[leaf], imags.at[leaf], sems.at[1, leaf]),
        )

    load_charges.start()
    for leaf in range(LEAVES_AHEAD):
        for copy in loads(leaf):
            copy.start()

    at_row = lax.rem(lax.axis_index("cone"), ROW)
    for listed in (inner, beside, wrapping):
        listed[0] = 0

    @pl.loop(0, count * 4)
    def _(pair):
        at = place_of(neighbours, pair)
        low, high = at < count, at >= 2 * count
        wraps = (low & (at_row == 0)) | (high & (at_row == ROW - 1))

        def put(listed):
            length = listed[0] + 1
            listed[0] = length
            listed[length] = pair

        @pl.when(jnp.logical_not(low | high))
        def _():
            put(inner)

        @pl.when(wraps)
        def _():
            put(wrapping)

        @pl.when((low | high) & jnp.logical_not(wraps))
        def _():
            put(beside)

    loaded[0] = 0

    @pl.loop(0, count)
    def _(leaf):
        sums[leaf] = jnp.zeros(sums.shape[1:], F32)

    load_charges.wait()

    def ready(leaf):
        @pl.loop(loaded[0], leaf + 1)
        def _(waited):
            for copy in loads(waited):
                copy.wait()

            @pl.when(waited + LEAVES_AHEAD < count)
            def _():
                for copy in loads(waited + LEAVES_AHEAD):
                    copy.start()

        loaded[0] = jnp.maximum(loaded[0], leaf + 1)

    def charge_of(pair):
        return charges[place_of(neighbours, pair) - count]

    listed_pairs(inner, reals, imags, charge_of, sums, ready)
    load_basis.start()
    ready(count - 1)
    load_basis.wait()


def own_sums(neighbours, near_real, near_imag, basis, own, ties):
    count = own.shape[0]
    pairs = jax.ShapeDtypeStruct((1 + PAIRS,), jnp.int32)

    def kernel(*refs):
        own_kernel(len(ties), *refs)

    return pl.pallas_call(
        kernel,
        out_shape=(
            pltpu.VMEM(near_real.shape, BF16),
            pltpu.VMEM(near_imag.shape, BF16),
            pltpu.VMEM(basis.shape, BF16),
            pltpu.VMEM(own.shape, F32),
            pairs,
            pairs,
        ),
        in_specs=[IN_SMEM] + [IN_HBM] * 4 + [ANYWHERE] * len(ties),
        out_specs=(IN_VMEM,) * 4 + (IN_SMEM,) * 2,
        scratch_shapes=[
            pltpu.SMEM(pairs.shape, jnp.int32),
            pltpu.VMEM(own.shape, BF16),
            pltpu.SMEM((1,), jnp.int32),
            pltpu.SemaphoreType.DMA((2, count)),
            pltpu.SemaphoreType.DMA((2,)),
        ],
        compiler_params=limit(6),
        cost_estimate=SMALL,
        name="own_sums",
    )(neighbours, *[kept_in_hbm(a) for a in (near_real, near_imag, basis, own)], *ties)


def more_kernel(parts, ties, neighbours, listed, reals, imags, *refs):
    sources = refs[:parts]
    token, sums, charges, sems = refs[parts + 1 + ties :]
    count = reals.shape[0]
    token[0] = 0

    @pl.when(listed[0] > 0)
    def _():
        copies = [
            pltpu.make_async_copy(source, charges.at[pl.ds(i * count, count)], sems.at[i])
            for i, source in enumerate(sources)
        ]
        for copy in copies:
            copy.start()
        for copy in copies:
            copy.wait()

    def charge_of(pair):
        at = place_of(neighbours, pair)
        inside = lax.rem(at, count)
        return charges[inside if parts == 1 else jnp.where(at < count, inside, inside + count)]

    listed_pairs(listed, reals, imags, charge_of, sums)


def more_sums(neighbours, listed, reals, imags, sources, sums, ties=()):
    parts = len(sources)

    def kernel(*refs):
        more_kernel(parts, len(ties), *refs)

    return pl.pallas_call(
        kernel,
        out_shape=(jax.ShapeDtypeStruct(listed.shape, jnp.int32), pltpu.VMEM(sums.shape, F32)),
        in_specs=[IN_SMEM] * 2 + [IN_VMEM] * 2 + [ANYWHERE] * parts + [IN_VMEM] + [ANYWHERE] * len(ties),
        out_specs=(IN_SMEM, IN_VMEM),
        input_output_aliases={4 + parts: 1},
        scratch_shapes=[
            pltpu.VMEM((parts * sums.shape[0],) + sums.shape[1:], BF16),
            pltpu.SemaphoreType.DMA((parts,)),
        ],
        compiler_params=limit(8),
        cost_estimate=SMALL,
        name="more_sums",
    )(neighbours, listed, reals, imags, *sources, sums, *ties)


def apply_kernel(sums, basis, leaf00, leaf01, leaf1, leaf2, out, totals, sems):
    count = sums.shape[0]

    def store(leaf):
        return pltpu.make_async_copy(totals.at[leaf], out.at[leaf], sems.at[leaf])

    for j, own in enumerate((leaf00, leaf01)):

        @pl.loop(0, count // 4)
        def _(half):
            for i in range(2):
                o = 2 * half + i
                leaf = j * (count // 2) + o
                coef = own[o].astype(F32) + leaf1[1 - j, o].astype(F32) + leaf2[j, o].astype(F32)
                coef = coef.astype(BF16)
                far = [jnp.dot(basis[leaf, s], coef, preferred_element_type=F32) for s in range(2)]
                totals[leaf] = (sums[leaf] + jnp.concatenate(far, axis=1)).astype(BF16)
                store(leaf).start()

    for leaf in range(count):
        store(leaf).wait()


def apply_leaves(sums, basis, leaf_terms):
    count = sums.shape[0]
    leaf_terms = leaf_terms[:2] + [kept_in_vmem(a) for a in leaf_terms[2:]]
    return pl.pallas_call(
        apply_kernel,
        out_shape=jax.ShapeDtypeStruct(sums.shape, BF16),
        in_specs=[IN_VMEM] * 6,
        out_specs=IN_HBM,
        scratch_shapes=[pltpu.VMEM(sums.shape, BF16), pltpu.SemaphoreType.DMA((count,))],
        compiler_params=limit(4),
        cost_estimate=SMALL,
        name="apply_leaves",
    )(sums, basis, *leaf_terms)


def per_device(
    upper_coef, phase, cone_used, transfer, leaf_basis, charges, neighbours, near_real, near_imag
):
    columns = upper_coef.shape[-1]
    coef = upper_coef.reshape(2, 4, 2, -1, columns)
    angle = phase.transpose(1, 2, 0).reshape(ANGLES, -1)
    to_z, to_both, to_core, kept, matrices = stage(angle, cone_used.T, coef, transfer)
    from_core = permute(to_core, FLIP_CORE)
    from_z = permute(to_z, FLIP_Z)
    from_both = permute(to_both, FLIP_BOTH)

    below = permute(charges, UP)
    above = permute(charges, DOWN)
    neighbours = neighbours.T
    transfer_outer = permute(tied(matrices, from_core), FLIP_OUTER)
    reals, imags, basis, sums, beside, wrapping = own_sums(
        neighbours, near_real, near_imag, leaf_basis, charges, [from_core]
    )
    token = beside
    kept_matrices = tied(matrices, token)
    transfer_core = permute(kept_matrices, FLIP_CORE)
    transfer_both = permute(tied(transfer_outer, token), FLIP_CORE)
    moves = [kept_matrices, transfer_core, transfer_outer, transfer_both]
    coefs = [kept, from_core, from_z, from_both]
    crossing = crossing_charges(below, above, [token])
    token, sums = more_sums(neighbours, beside, reals, imags, [below, above], sums)
    crossing = tied(crossing, from_z, from_both, transfer_core, transfer_both, token)
    wrapped = permute(crossing, NEXT_ROW)

    far_first, far_second = transfer_terms([2], coefs, moves, [crossing])
    up = permute(far_first, X_UP)
    down = permute(far_second, X_DOWN)
    up_first, up_second, down_first, down_second = transfer_terms([1, 3], coefs, moves)
    to_above = with_arrived(up_second, up_first, up)
    to_below = with_arrived(down_first, down_second, down)
    from_below = permute(to_above, X_UP)
    from_above = permute(to_below, X_DOWN)
    own_first, own_second = transfer_terms([0], coefs, moves, [to_above, to_below])
    _, sums = more_sums(neighbours, wrapping, reals, imags, [wrapped], sums, [own_first])
    return apply_leaves(sums, basis, [own_first, own_second, from_below, from_above])


def solution(mesh):
    in_specs = (
        P("cluster", "cone", None, None),
        P("cluster", "cone", None),
        P("cluster", "cone"),
        P("cone", None, None, None),
        P(("cluster", "cone"), None, None, None),
        P(("cluster", "cone"), None, None),
        P(("cluster", "cone"), None),
        P(("cluster", "cone"), None, None, None),
        P(("cluster", "cone"), None, None, None),
    )
    out_specs = P(("cluster", "cone"), None, None)
    return jax.shard_map(
        per_device, mesh=mesh, in_specs=in_specs, out_specs=out_specs, check_vma=False
    )
```

```python
import jax
import jax.numpy as jnp
from jax import lax
from jax.experimental import pallas as pl
from jax.experimental.pallas import tpu as pltpu
from jax.sharding import PartitionSpec as P

AXES = ("cluster", "cone")
DEVICES = 128
ROW = 8
F32 = jnp.float32
BF16 = jnp.bfloat16
SMALL = pl.CostEstimate(flops=0, bytes_accessed=1024, transcendentals=0)


def moved(dx):
    return [(d, (d & ~6) | ((((d >> 1) & 3) + dx) % 4) << 1) for d in range(DEVICES)]


FLIP_CORE = [(d, d ^ 1) for d in range(DEVICES)]
FLIP_Z = [(d, d ^ 8) for d in range(DEVICES)]
FLIP_BOTH = [(d, d ^ 9) for d in range(DEVICES)]
FLIP_OUTER = [(d, d ^ 72) for d in range(DEVICES)]
X_UP = moved(1)
X_DOWN = moved(-1)
UP = [(d, d - d % ROW + (d + 1) % ROW) for d in range(DEVICES)]
DOWN = [(d, d - d % ROW + (d - 1) % ROW) for d in range(DEVICES)]
NEXT_ROW = [(d, d + ROW) for d in range(0, DEVICES - ROW, ROW)] + [
    (d, d - ROW) for d in range(2 * ROW - 1, DEVICES, ROW)
]


def permute(array, pairs):
    return lax.ppermute(array, AXES, pairs)


IN_VMEM = pl.BlockSpec(memory_space=pltpu.VMEM)
IN_HBM = pl.BlockSpec(memory_space=pltpu.HBM)
IN_SMEM = pl.BlockSpec(memory_space=pltpu.SMEM)
ANYWHERE = pl.BlockSpec(memory_space=pl.ANY)


def kept_in_hbm(array):
    return pltpu.with_memory_space_constraint(array, pltpu.HBM)


def kept_in_vmem(array):
    return pltpu.with_memory_space_constraint(array, pltpu.VMEM)


def limit(mib):
    return pltpu.CompilerParams(vmem_limit_bytes=mib << 20)


ANGLES = 16
TAIL = ANGLES


def stage_kernel(angle, used, coef, transfer, *refs):
    outs, buffers, angles, weights, sems = refs[:5], refs[5:10], refs[10], refs[11], refs[12]
    small = [pltpu.make_async_copy(angle, angles, sems.at[1, 5]), pltpu.make_async_copy(used, weights, sems.at[1, 6])]
    for copy in small:
        copy.start()
    cone = lax.axis_index("cone")
    zl, core = cone // 8, cone % 2
    sources = ((1 - zl, core), (1 - zl, 1 - core), (zl, 1 - core), (zl, core))
    rows = coef.shape[-2]
    loads = [
        [
            pltpu.make_async_copy(coef.at[z, x, c], buffers[i].at[pl.ds(x * rows, rows)], sems.at[0, i * 4 + x])
            for x in range(4)
        ]
        for i, (z, c) in enumerate(sources)
    ] + [[pltpu.make_async_copy(transfer, buffers[4], sems.at[0, 16])]]
    stores = [pltpu.make_async_copy(buffers[i], outs[i], sems.at[1, i]) for i in range(5)]
    for part in loads:
        for load in part:
            load.start()

    for copy in small:
        copy.wait()
    high = angles[...].astype(BF16)
    left = angles[...] - high.astype(F32)
    middle = left.astype(BF16)
    low = (left - middle.astype(F32)).astype(BF16)
    weight = weights[...].astype(F32)
    each = (ANGLES // 2, weight.shape[1])
    weight = jnp.concatenate([jnp.broadcast_to(weight[i : i + 1], each) for i in range(2)], axis=0)
    pieces = [piece.astype(F32) for piece in (high, middle, low)] + [weight]
    tail = jnp.concatenate(pieces, axis=1).astype(BF16)
    for buffer in buffers[:4]:
        buffer[4 * rows :, :] = tail

    for part, store in zip(loads, stores):
        for load in part:
            load.wait()
        store.start()
    for store in stores:
        store.wait()


def stage(angle, used, coef, transfer):
    part = jax.ShapeDtypeStruct((4 * coef.shape[-2] + TAIL, coef.shape[-1]), coef.dtype)
    outs = (part,) * 4 + (jax.ShapeDtypeStruct(transfer.shape, transfer.dtype),)
    return pl.pallas_call(
        stage_kernel,
        out_shape=outs,
        in_specs=[IN_HBM] * 4,
        out_specs=(IN_HBM,) * 5,
        scratch_shapes=[pltpu.VMEM(a.shape, a.dtype) for a in (*outs, angle, used)]
        + [pltpu.SemaphoreType.DMA((2, 17))],
        compiler_params=limit(5),
        cost_estimate=SMALL,
        name="stage",
    )(*[kept_in_hbm(a) for a in (angle, used, coef, transfer)])


def tied(array, *others):
    def kernel(*refs):
        del refs

    return pl.pallas_call(
        kernel,
        out_shape=jax.ShapeDtypeStruct(array.shape, array.dtype),
        in_specs=[ANYWHERE] * (1 + len(others)),
        out_specs=ANYWHERE,
        input_output_aliases={0: 0},
        compiler_params=limit(1),
        cost_estimate=SMALL,
        name="tied",
    )(array, *others)


def cross_kernel(ties, below, above, *refs):
    out, buffer, sem = refs[ties:]
    at_row = lax.rem(lax.axis_index("cone"), ROW)

    def carry(source):
        for copy in (pltpu.make_async_copy(source, buffer, sem), pltpu.make_async_copy(buffer, out, sem)):
            copy.start()
            copy.wait()

    @pl.when(at_row == 0)
    def _():
        carry(below)

    @pl.when(at_row == ROW - 1)
    def _():
        carry(above)


def crossing_charges(below, above, ties):
    def kernel(*refs):
        cross_kernel(len(ties), *refs)

    return pl.pallas_call(
        kernel,
        out_shape=jax.ShapeDtypeStruct(below.shape, below.dtype),
        in_specs=[ANYWHERE] * (2 + len(ties)),
        out_specs=ANYWHERE,
        scratch_shapes=[pltpu.VMEM(below.shape, below.dtype), pltpu.SemaphoreType.DMA],
        compiler_params=limit(3),
        cost_estimate=SMALL,
        name="crossing_charges",
    )(below, above, *ties)


def transfer_kernel(offsets, ties, *refs):
    coefs, moves, outs = refs[:4], refs[4:8], refs[8 + ties :]
    cone_index = lax.axis_index("cone")
    zl, x, core = cone_index // 8, (cone_index // 2) % 4, cone_index % 2
    size, width = outs[0].shape[1:]
    half = size // 2
    clusters = width // 4
    lanes = lax.broadcasted_iota(jnp.int32, (ANGLES, clusters), 1)
    turns = []
    for coef in coefs:
        tail = coef[coef.shape[0] - TAIL :, :].astype(F32)
        high, middle, low, weight = (tail[:, i * clusters : (i + 1) * clusters] for i in range(4))
        angle = high + middle + low
        turns.append((jnp.cos(angle) * weight, jnp.sin(angle) * weight))

    for t, offset in enumerate(offsets):
        target = (x + offset) % 4
        first = zl * 16 + target * 4 + core * 2
        columns_of = [
            [
                [
                    jnp.sum(jnp.where(lanes == first + j, part, 0.0), axis=1, keepdims=True)
                    for part in turns[source]
                ]
                for j in range(2)
            ]
            for source in range(4)
        ]
        for o in range(8):
            total = None
            for source in range(4):
                columns = []
                for j in range(2):
                    rows = []
                    for cone in range(2):
                        at = cone * 8 + o
                        cosine, sine = (column[at : at + 1] for column in columns_of[source][j])
                        start = pl.multiple_of(((target * 2 + j) * 2 + cone) * size, size)
                        real = coefs[source][pl.ds(start, half), :].astype(F32)
                        imag = coefs[source][pl.ds(start + half, half), :].astype(F32)
                        rows.append((cosine * real - sine * imag).astype(BF16))
                        rows.append((sine * real + cosine * imag).astype(BF16))
                    columns.append(jnp.concatenate(rows, axis=0))
                turned = jnp.concatenate(columns, axis=1)
                matrix = jnp.concatenate([moves[source][0, o], moves[source][1, o]], axis=1)
                term = jnp.dot(matrix, turned, preferred_element_type=F32)
                total = term if total is None else total + term
            for j in range(2):
                outs[t * 2 + j][o] = total[:, j * width : (j + 1) * width].astype(BF16)


def transfer_terms(offsets, coefs, moves, ties=()):
    out = pltpu.VMEM(moves[0].shape[1:], BF16)

    def kernel(*refs):
        transfer_kernel(offsets, len(ties), *refs)

    return pl.pallas_call(
        kernel,
        out_shape=(out,) * (2 * len(offsets)),
        in_specs=[IN_VMEM] * 8 + [ANYWHERE] * len(ties),
        out_specs=(IN_VMEM,) * (2 * len(offsets)),
        compiler_params=limit(8),
        cost_estimate=SMALL,
        name="transfer_terms",
    )(*[kept_in_vmem(a) for a in coefs], *[kept_in_vmem(a) for a in moves], *ties)


def add_kernel(left, right, arrived, *rest):
    out = rest[-1]
    for o in range(8):
        out[0, o] = left[o]
        out[1, o] = (right[o].astype(F32) + arrived[o].astype(F32)).astype(BF16)


def with_arrived(left, right, arrived, ties=()):
    return pl.pallas_call(
        add_kernel,
        out_shape=pltpu.VMEM((2,) + left.shape, BF16),
        in_specs=[IN_VMEM] * 3 + [ANYWHERE] * len(ties),
        out_specs=IN_VMEM,
        compiler_params=limit(2),
        cost_estimate=SMALL,
        name="with_arrived",
    )(left, right, kept_in_vmem(arrived), *ties)


def pair_term(real, imag, charge):
    points, columns = charge.shape[0], charge.shape[1] // 2
    both = jnp.dot(jnp.concatenate([real, imag], axis=0), charge, preferred_element_type=F32)
    first, second = both[:points], both[points:]
    return jnp.concatenate(
        [first[:, :columns] - second[:, columns:], first[:, columns:] + second[:, :columns]], axis=1
    )


GROUP = 4
PAIRS = 64
PLACES = 32


def place_of(neighbours, pair):
    count = neighbours.shape[1]
    device = lax.axis_index("cluster") * 16 + lax.axis_index("cone")
    return neighbours[pair % 4, pair // 4] - (device - 1) * count


def listed_pairs(listed, reals, imags, charges, sums, ready=None):
    length = listed[0]

    @pl.loop(0, (length + GROUP - 1) // GROUP)
    def _(group):
        places = [group * GROUP + i for i in range(GROUP)]
        entries = [listed[1 + jnp.minimum(place, length - 1)] for place in places]
        if ready is not None:
            ready(entries[-1] // (4 * PLACES))
        terms = []
        for place, entry in zip(places, entries):
            charge = charges[entry % PLACES]
            charge = jnp.where(place < length, charge, jnp.zeros_like(charge))
            leaf, n = entry // (4 * PLACES), (entry // PLACES) % 4
            terms.append((leaf, pair_term(reals[leaf, n], imags[leaf, n], charge)))
        for leaf, term in terms:
            sums[leaf] += term


LEAVES_AHEAD = 5


def own_kernel(
    ties, neighbours, near_real, near_imag, basis, own, *refs
):
    reals, imags, bases, sums, beside, wrapping, inner, charges, loaded, sems, other_sems = refs[ties:]
    count = own.shape[0]
    load_charges = pltpu.make_async_copy(own, charges, other_sems.at[0])
    load_basis = pltpu.make_async_copy(basis, bases, other_sems.at[1])

    def loads(leaf):
        return (
            pltpu.make_async_copy(near_real.at[leaf], reals.at[leaf], sems.at[0, leaf]),
            pltpu.make_async_copy(near_imag.at[leaf], imags.at[leaf], sems.at[1, leaf]),
        )

    load_charges.start()
    for leaf in range(LEAVES_AHEAD):
        for copy in loads(leaf):
            copy.start()

    at_row = lax.rem(lax.axis_index("cone"), ROW)
    for listed in (inner, beside, wrapping):
        listed[0] = 0

    @pl.loop(0, count * 4)
    def _(pair):
        at = place_of(neighbours, pair)
        low, high = at < count, at >= 2 * count
        wraps = (low & (at_row == 0)) | (high & (at_row == ROW - 1))

        inside = lax.rem(at, count)

        def put(listed, charges_at):
            length = listed[0] + 1
            listed[0] = length
            listed[length] = pair * PLACES + charges_at

        @pl.when(jnp.logical_not(low | high))
        def _():
            put(inner, inside)

        @pl.when(wraps)
        def _():
            put(wrapping, inside)

        @pl.when((low | high) & jnp.logical_not(wraps))
        def _():
            put(beside, jnp.where(low, inside, inside + count))

    loaded[0] = 0

    @pl.loop(0, count)
    def _(leaf):
        sums[leaf] = jnp.zeros(sums.shape[1:], F32)

    load_charges.wait()

    def ready(leaf):
        @pl.loop(loaded[0], leaf + 1)
        def _(waited):
            for copy in loads(waited):
                copy.wait()

            @pl.when(waited + LEAVES_AHEAD < count)
            def _():
                for copy in loads(waited + LEAVES_AHEAD):
                    copy.start()

        loaded[0] = jnp.maximum(loaded[0], leaf + 1)

    listed_pairs(inner, reals, imags, charges, sums, ready)
    load_basis.start()
    ready(count - 1)
    load_basis.wait()


def own_sums(neighbours, near_real, near_imag, basis, own, ties):
    count = own.shape[0]
    pairs = jax.ShapeDtypeStruct((1 + PAIRS,), jnp.int32)

    def kernel(*refs):
        own_kernel(len(ties), *refs)

    return pl.pallas_call(
        kernel,
        out_shape=(
            pltpu.VMEM(near_real.shape, BF16),
            pltpu.VMEM(near_imag.shape, BF16),
            pltpu.VMEM(basis.shape, BF16),
            pltpu.VMEM(own.shape, F32),
            pairs,
            pairs,
        ),
        in_specs=[IN_SMEM] + [IN_HBM] * 4 + [ANYWHERE] * len(ties),
        out_specs=(IN_VMEM,) * 4 + (IN_SMEM,) * 2,
        scratch_shapes=[
            pltpu.SMEM(pairs.shape, jnp.int32),
            pltpu.VMEM(own.shape, BF16),
            pltpu.SMEM((1,), jnp.int32),
            pltpu.SemaphoreType.DMA((2, count)),
            pltpu.SemaphoreType.DMA((2,)),
        ],
        compiler_params=limit(6),
        cost_estimate=SMALL,
        name="own_sums",
    )(neighbours, *[kept_in_hbm(a) for a in (near_real, near_imag, basis, own)], *ties)


def more_kernel(parts, ties, listed, reals, imags, *refs):
    sources = refs[:parts]
    token, sums, charges, sems = refs[parts + 1 + ties :]
    count = reals.shape[0]
    token[0] = 0

    @pl.when(listed[0] > 0)
    def _():
        copies = [
            pltpu.make_async_copy(source, charges.at[pl.ds(i * count, count)], sems.at[i])
            for i, source in enumerate(sources)
        ]
        for copy in copies:
            copy.start()
        for copy in copies:
            copy.wait()

    listed_pairs(listed, reals, imags, charges, sums)


def more_sums(listed, reals, imags, sources, sums, ties=()):
    parts = len(sources)

    def kernel(*refs):
        more_kernel(parts, len(ties), *refs)

    return pl.pallas_call(
        kernel,
        out_shape=(jax.ShapeDtypeStruct(listed.shape, jnp.int32), pltpu.VMEM(sums.shape, F32)),
        in_specs=[IN_SMEM] + [IN_VMEM] * 2 + [ANYWHERE] * parts + [IN_VMEM] + [ANYWHERE] * len(ties),
        out_specs=(IN_SMEM, IN_VMEM),
        input_output_aliases={3 + parts: 1},
        scratch_shapes=[
            pltpu.VMEM((parts * sums.shape[0],) + sums.shape[1:], BF16),
            pltpu.SemaphoreType.DMA((parts,)),
        ],
        compiler_params=limit(8),
        cost_estimate=SMALL,
        name="more_sums",
    )(listed, reals, imags, *sources, sums, *ties)


def apply_kernel(sums, basis, leaf00, leaf01, leaf1, leaf2, out, totals, sems):
    count = sums.shape[0]

    def store(leaf):
        return pltpu.make_async_copy(totals.at[leaf], out.at[leaf], sems.at[leaf])

    for j, own in enumerate((leaf00, leaf01)):

        @pl.loop(0, count // 8)
        def _(part):
            for i in range(4):
                o = 4 * part + i
                leaf = j * (count // 2) + o
                coef = own[o].astype(F32) + leaf1[1 - j, o].astype(F32) + leaf2[j, o].astype(F32)
                coef = coef.astype(BF16)
                far = [jnp.dot(basis[leaf, s], coef, preferred_element_type=F32) for s in range(2)]
                totals[leaf] = (sums[leaf] + jnp.concatenate(far, axis=1)).astype(BF16)
                store(leaf).start()

    for leaf in range(count):
        store(leaf).wait()


def apply_leaves(sums, basis, leaf_terms):
    count = sums.shape[0]
    leaf_terms = leaf_terms[:2] + [kept_in_vmem(a) for a in leaf_terms[2:]]
    return pl.pallas_call(
        apply_kernel,
        out_shape=jax.ShapeDtypeStruct(sums.shape, BF16),
        in_specs=[IN_VMEM] * 6,
        out_specs=IN_HBM,
        scratch_shapes=[pltpu.VMEM(sums.shape, BF16), pltpu.SemaphoreType.DMA((count,))],
        compiler_params=limit(4),
        cost_estimate=SMALL,
        name="apply_leaves",
    )(sums, basis, *leaf_terms)


def per_device(
    upper_coef, phase, cone_used, transfer, leaf_basis, charges, neighbours, near_real, near_imag
):
    columns = upper_coef.shape[-1]
    coef = upper_coef.reshape(2, 4, 2, -1, columns)
    angle = phase.transpose(1, 2, 0).reshape(ANGLES, -1)
    to_z, to_both, to_core, kept, matrices = stage(angle, cone_used.T, coef, transfer)
    from_core = permute(to_core, FLIP_CORE)
    from_z = permute(to_z, FLIP_Z)
    from_both = permute(to_both, FLIP_BOTH)

    below = permute(charges, UP)
    above = permute(charges, DOWN)
    neighbours = neighbours.T
    transfer_outer = permute(tied(matrices, from_core), FLIP_OUTER)
    reals, imags, basis, sums, beside, wrapping = own_sums(
        neighbours, near_real, near_imag, leaf_basis, charges, [from_core]
    )
    token = beside
    kept_matrices = tied(matrices, token)
    transfer_core = permute(kept_matrices, FLIP_CORE)
    transfer_both = permute(tied(transfer_outer, token), FLIP_CORE)
    moves = [kept_matrices, transfer_core, transfer_outer, transfer_both]
    coefs = [kept, from_core, from_z, from_both]
    crossing = crossing_charges(below, above, [token])
    token, sums = more_sums(beside, reals, imags, [below, above], sums)
    crossing = tied(crossing, from_z, from_both, transfer_core, transfer_both, token)
    wrapped = permute(crossing, NEXT_ROW)

    far_first, far_second = transfer_terms([2], coefs, moves, [crossing])
    up = permute(far_first, X_UP)
    down = permute(far_second, X_DOWN)
    up_first, up_second, down_first, down_second = transfer_terms([1, 3], coefs, moves)
    to_above = with_arrived(up_second, up_first, up)
    to_below = with_arrived(down_first, down_second, down)
    from_below = permute(to_above, X_UP)
    from_above = permute(to_below, X_DOWN)
    own_first, own_second = transfer_terms([0], coefs, moves, [to_above, to_below])
    _, sums = more_sums(wrapping, reals, imags, [wrapped], sums, [own_first])
    return apply_leaves(sums, basis, [own_first, own_second, from_below, from_above])


def solution(mesh):
    in_specs = (
        P("cluster", "cone", None, None),
        P("cluster", "cone", None),
        P("cluster", "cone"),
        P("cone", None, None, None),
        P(("cluster", "cone"), None, None, None),
        P(("cluster", "cone"), None, None),
        P(("cluster", "cone"), None),
        P(("cluster", "cone"), None, None, None),
        P(("cluster", "cone"), None, None, None),
    )
    out_specs = P(("cluster", "cone"), None, None)
    return jax.shard_map(
        per_device, mesh=mesh, in_specs=in_specs, out_specs=out_specs, check_vma=False
    )
```

```python
import jax
import jax.numpy as jnp
from jax import lax
from jax.experimental import pallas as pl
from jax.experimental.pallas import tpu as pltpu
from jax.sharding import PartitionSpec as P

AXES = ("cluster", "cone")
DEVICES = 128
ROW = 8
F32 = jnp.float32
BF16 = jnp.bfloat16
SMALL = pl.CostEstimate(flops=0, bytes_accessed=1024, transcendentals=0)


def moved(dx):
    return [(d, (d & ~6) | ((((d >> 1) & 3) + dx) % 4) << 1) for d in range(DEVICES)]


FLIP_CORE = [(d, d ^ 1) for d in range(DEVICES)]
FLIP_Z = [(d, d ^ 8) for d in range(DEVICES)]
FLIP_BOTH = [(d, d ^ 9) for d in range(DEVICES)]
FLIP_OUTER = [(d, d ^ 72) for d in range(DEVICES)]
X_UP = moved(1)
X_DOWN = moved(-1)
UP = [(d, d - d % ROW + (d + 1) % ROW) for d in range(DEVICES)]
DOWN = [(d, d - d % ROW + (d - 1) % ROW) for d in range(DEVICES)]
NEXT_ROW = [(d, d + ROW) for d in range(0, DEVICES - ROW, ROW)] + [
    (d, d - ROW) for d in range(2 * ROW - 1, DEVICES, ROW)
]


def permute(array, pairs):
    return lax.ppermute(array, AXES, pairs)


IN_VMEM = pl.BlockSpec(memory_space=pltpu.VMEM)
IN_HBM = pl.BlockSpec(memory_space=pltpu.HBM)
IN_SMEM = pl.BlockSpec(memory_space=pltpu.SMEM)
ANYWHERE = pl.BlockSpec(memory_space=pl.ANY)


def kept_in_hbm(array):
    return pltpu.with_memory_space_constraint(array, pltpu.HBM)


def kept_in_vmem(array):
    return pltpu.with_memory_space_constraint(array, pltpu.VMEM)


def limit(mib):
    return pltpu.CompilerParams(vmem_limit_bytes=mib << 20)


ANGLES = 16
TAIL = ANGLES


def stage_kernel(angle, used, coef, transfer, *refs):
    outs, buffers, angles, weights, sems = refs[:5], refs[5:10], refs[10], refs[11], refs[12]
    small = [pltpu.make_async_copy(angle, angles, sems.at[1, 5]), pltpu.make_async_copy(used, weights, sems.at[1, 6])]
    for copy in small:
        copy.start()
    cone = lax.axis_index("cone")
    zl, core = cone // 8, cone % 2
    sources = ((1 - zl, core), (1 - zl, 1 - core), (zl, 1 - core), (zl, core))
    rows = coef.shape[-2]
    loads = [
        [
            pltpu.make_async_copy(coef.at[z, x, c], buffers[i].at[pl.ds(x * rows, rows)], sems.at[0, i * 4 + x])
            for x in range(4)
        ]
        for i, (z, c) in enumerate(sources)
    ] + [[pltpu.make_async_copy(transfer, buffers[4], sems.at[0, 16])]]
    stores = [pltpu.make_async_copy(buffers[i], outs[i], sems.at[1, i]) for i in range(5)]
    for part in loads:
        for load in part:
            load.start()

    for copy in small:
        copy.wait()
    high = angles[...].astype(BF16)
    left = angles[...] - high.astype(F32)
    middle = left.astype(BF16)
    low = (left - middle.astype(F32)).astype(BF16)
    weight = weights[...].astype(F32)
    each = (ANGLES // 2, weight.shape[1])
    weight = jnp.concatenate([jnp.broadcast_to(weight[i : i + 1], each) for i in range(2)], axis=0)
    pieces = [piece.astype(F32) for piece in (high, middle, low)] + [weight]
    tail = jnp.concatenate(pieces, axis=1).astype(BF16)
    for buffer in buffers[:4]:
        buffer[4 * rows :, :] = tail

    for part, store in zip(loads, stores):
        for load in part:
            load.wait()
        store.start()
    for store in stores:
        store.wait()


def stage(angle, used, coef, transfer):
    part = jax.ShapeDtypeStruct((4 * coef.shape[-2] + TAIL, coef.shape[-1]), coef.dtype)
    outs = (part,) * 4 + (jax.ShapeDtypeStruct(transfer.shape, transfer.dtype),)
    return pl.pallas_call(
        stage_kernel,
        out_shape=outs,
        in_specs=[IN_HBM] * 4,
        out_specs=(IN_HBM,) * 5,
        scratch_shapes=[pltpu.VMEM(a.shape, a.dtype) for a in (*outs, angle, used)]
        + [pltpu.SemaphoreType.DMA((2, 17))],
        compiler_params=limit(5),
        cost_estimate=SMALL,
        name="stage",
    )(*[kept_in_hbm(a) for a in (angle, used, coef, transfer)])


def tied(array, *others):
    def kernel(*refs):
        del refs

    return pl.pallas_call(
        kernel,
        out_shape=jax.ShapeDtypeStruct(array.shape, array.dtype),
        in_specs=[ANYWHERE] * (1 + len(others)),
        out_specs=ANYWHERE,
        input_output_aliases={0: 0},
        compiler_params=limit(1),
        cost_estimate=SMALL,
        name="tied",
    )(array, *others)


def cross_kernel(ties, below, above, *refs):
    out, buffer, sem = refs[ties:]
    at_row = lax.rem(lax.axis_index("cone"), ROW)

    def carry(source):
        for copy in (pltpu.make_async_copy(source, buffer, sem), pltpu.make_async_copy(buffer, out, sem)):
            copy.start()
            copy.wait()

    @pl.when(at_row == 0)
    def _():
        carry(below)

    @pl.when(at_row == ROW - 1)
    def _():
        carry(above)


def crossing_charges(below, above, ties):
    def kernel(*refs):
        cross_kernel(len(ties), *refs)

    return pl.pallas_call(
        kernel,
        out_shape=jax.ShapeDtypeStruct(below.shape, below.dtype),
        in_specs=[ANYWHERE] * (2 + len(ties)),
        out_specs=ANYWHERE,
        scratch_shapes=[pltpu.VMEM(below.shape, below.dtype), pltpu.SemaphoreType.DMA],
        compiler_params=limit(3),
        cost_estimate=SMALL,
        name="crossing_charges",
    )(below, above, *ties)


def transfer_kernel(offsets, ties, *refs):
    coefs, moves, outs = refs[:4], refs[4:8], refs[8 + ties :]
    cone_index = lax.axis_index("cone")
    zl, x, core = cone_index // 8, (cone_index // 2) % 4, cone_index % 2
    size, width = outs[0].shape[1:]
    half = size // 2
    clusters = width // 4
    lanes = lax.broadcasted_iota(jnp.int32, (ANGLES, clusters), 1)
    turns = []
    for coef in coefs:
        tail = coef[coef.shape[0] - TAIL :, :].astype(F32)
        high, middle, low, weight = (tail[:, i * clusters : (i + 1) * clusters] for i in range(4))
        angle = high + middle + low
        turns.append((jnp.cos(angle) * weight, jnp.sin(angle) * weight))

    for t, offset in enumerate(offsets):
        target = (x + offset) % 4
        first = zl * 16 + target * 4 + core * 2
        columns_of = [
            [
                [
                    jnp.sum(jnp.where(lanes == first + j, part, 0.0), axis=1, keepdims=True)
                    for part in turns[source]
                ]
                for j in range(2)
            ]
            for source in range(4)
        ]
        for o in range(8):
            total = None
            for source in range(4):
                columns = []
                for j in range(2):
                    rows = []
                    for cone in range(2):
                        at = cone * 8 + o
                        cosine, sine = (column[at : at + 1] for column in columns_of[source][j])
                        start = pl.multiple_of(((target * 2 + j) * 2 + cone) * size, size)
                        real = coefs[source][pl.ds(start, half), :].astype(F32)
                        imag = coefs[source][pl.ds(start + half, half), :].astype(F32)
                        rows.append((cosine * real - sine * imag).astype(BF16))
                        rows.append((sine * real + cosine * imag).astype(BF16))
                    columns.append(jnp.concatenate(rows, axis=0))
                turned = jnp.concatenate(columns, axis=1)
                matrix = jnp.concatenate([moves[source][0, o], moves[source][1, o]], axis=1)
                term = jnp.dot(matrix, turned, preferred_element_type=F32)
                total = term if total is None else total + term
            for j in range(2):
                outs[t * 2 + j][o] = total[:, j * width : (j + 1) * width].astype(BF16)


def transfer_terms(offsets, coefs, moves, ties=()):
    out = pltpu.VMEM(moves[0].shape[1:], BF16)

    def kernel(*refs):
        transfer_kernel(offsets, len(ties), *refs)

    return pl.pallas_call(
        kernel,
        out_shape=(out,) * (2 * len(offsets)),
        in_specs=[IN_VMEM] * 8 + [ANYWHERE] * len(ties),
        out_specs=(IN_VMEM,) * (2 * len(offsets)),
        compiler_params=limit(8),
        cost_estimate=SMALL,
        name="transfer_terms",
    )(*[kept_in_vmem(a) for a in coefs], *[kept_in_vmem(a) for a in moves], *ties)


def add_kernel(left, right, arrived, *rest):
    out = rest[-1]
    for o in range(8):
        out[0, o] = left[o]
        out[1, o] = (right[o].astype(F32) + arrived[o].astype(F32)).astype(BF16)


def with_arrived(left, right, arrived, ties=()):
    return pl.pallas_call(
        add_kernel,
        out_shape=pltpu.VMEM((2,) + left.shape, BF16),
        in_specs=[IN_VMEM] * 3 + [ANYWHERE] * len(ties),
        out_specs=IN_VMEM,
        compiler_params=limit(2),
        cost_estimate=SMALL,
        name="with_arrived",
    )(left, right, kept_in_vmem(arrived), *ties)


def pair_term(real, imag, charge):
    points, columns = charge.shape[0], charge.shape[1] // 2
    both = jnp.dot(jnp.concatenate([real, imag], axis=0), charge, preferred_element_type=F32)
    first, second = both[:points], both[points:]
    return jnp.concatenate(
        [first[:, :columns] - second[:, columns:], first[:, columns:] + second[:, :columns]], axis=1
    )


GROUP = 8
PAIRS = 64
PLACES = 32


def place_of(neighbours, pair):
    count = neighbours.shape[1]
    device = lax.axis_index("cluster") * 16 + lax.axis_index("cone")
    return neighbours[pair % 4, pair // 4] - (device - 1) * count


def listed_pairs(listed, reals, imags, charges, sums, ready=None):
    length = listed[0]

    @pl.loop(0, (length + GROUP - 1) // GROUP)
    def _(group):
        places = [group * GROUP + i for i in range(GROUP)]
        entries = [listed[1 + jnp.minimum(place, length - 1)] for place in places]
        if ready is not None:
            ready(entries[-1] // (4 * PLACES))
        terms = []
        for place, entry in zip(places, entries):
            charge = charges[entry % PLACES]
            charge = jnp.where(place < length, charge, jnp.zeros_like(charge))
            leaf, n = entry // (4 * PLACES), (entry // PLACES) % 4
            terms.append((leaf, pair_term(reals[leaf, n], imags[leaf, n], charge)))
        for leaf, term in terms:
            sums[leaf] += term


LEAVES_AHEAD = 5


def own_kernel(
    ties, neighbours, near_real, near_imag, basis, own, *refs
):
    reals, imags, bases, sums, beside, wrapping, inner, charges, loaded, sems, other_sems = refs[ties:]
    count = own.shape[0]
    load_charges = pltpu.make_async_copy(own, charges, other_sems.at[0])
    load_basis = pltpu.make_async_copy(basis, bases, other_sems.at[1])

    def loads(leaf):
        return (
            pltpu.make_async_copy(near_real.at[leaf], reals.at[leaf], sems.at[0, leaf]),
            pltpu.make_async_copy(near_imag.at[leaf], imags.at[leaf], sems.at[1, leaf]),
        )

    load_charges.start()
    for leaf in range(LEAVES_AHEAD):
        for copy in loads(leaf):
            copy.start()

    at_row = lax.rem(lax.axis_index("cone"), ROW)
    for listed in (inner, beside, wrapping):
        listed[0] = 0

    @pl.loop(0, count * 4)
    def _(pair):
        at = place_of(neighbours, pair)
        low, high = at < count, at >= 2 * count
        wraps = (low & (at_row == 0)) | (high & (at_row == ROW - 1))

        inside = lax.rem(at, count)

        def put(listed, charges_at):
            length = listed[0] + 1
            listed[0] = length
            listed[length] = pair * PLACES + charges_at

        @pl.when(jnp.logical_not(low | high))
        def _():
            put(inner, inside)

        @pl.when(wraps)
        def _():
            put(wrapping, inside)

        @pl.when((low | high) & jnp.logical_not(wraps))
        def _():
            put(beside, jnp.where(low, inside, inside + count))

    loaded[0] = 0

    @pl.loop(0, count)
    def _(leaf):
        sums[leaf] = jnp.zeros(sums.shape[1:], F32)

    load_charges.wait()

    def ready(leaf):
        @pl.loop(loaded[0], leaf + 1)
        def _(waited):
            for copy in loads(waited):
                copy.wait()

            @pl.when(waited + LEAVES_AHEAD < count)
            def _():
                for copy in loads(waited + LEAVES_AHEAD):
                    copy.start()

        loaded[0] = jnp.maximum(loaded[0], leaf + 1)

    listed_pairs(inner, reals, imags, charges, sums, ready)
    load_basis.start()
    ready(count - 1)
    load_basis.wait()


def own_sums(neighbours, near_real, near_imag, basis, own, ties):
    count = own.shape[0]
    pairs = jax.ShapeDtypeStruct((1 + PAIRS,), jnp.int32)

    def kernel(*refs):
        own_kernel(len(ties), *refs)

    return pl.pallas_call(
        kernel,
        out_shape=(
            pltpu.VMEM(near_real.shape, BF16),
            pltpu.VMEM(near_imag.shape, BF16),
            pltpu.VMEM(basis.shape, BF16),
            pltpu.VMEM(own.shape, F32),
            pairs,
            pairs,
        ),
        in_specs=[IN_SMEM] + [IN_HBM] * 4 + [ANYWHERE] * len(ties),
        out_specs=(IN_VMEM,) * 4 + (IN_SMEM,) * 2,
        scratch_shapes=[
            pltpu.SMEM(pairs.shape, jnp.int32),
            pltpu.VMEM(own.shape, BF16),
            pltpu.SMEM((1,), jnp.int32),
            pltpu.SemaphoreType.DMA((2, count)),
            pltpu.SemaphoreType.DMA((2,)),
        ],
        compiler_params=limit(6),
        cost_estimate=SMALL,
        name="own_sums",
    )(neighbours, *[kept_in_hbm(a) for a in (near_real, near_imag, basis, own)], *ties)


def more_kernel(parts, ties, listed, reals, imags, *refs):
    sources = refs[:parts]
    token, sums, charges, sems = refs[parts + 1 + ties :]
    count = reals.shape[0]
    token[0] = 0

    @pl.when(listed[0] > 0)
    def _():
        copies = [
            pltpu.make_async_copy(source, charges.at[pl.ds(i * count, count)], sems.at[i])
            for i, source in enumerate(sources)
        ]
        for copy in copies:
            copy.start()
        for copy in copies:
            copy.wait()

    listed_pairs(listed, reals, imags, charges, sums)


def more_sums(listed, reals, imags, sources, sums, ties=()):
    parts = len(sources)

    def kernel(*refs):
        more_kernel(parts, len(ties), *refs)

    return pl.pallas_call(
        kernel,
        out_shape=(jax.ShapeDtypeStruct(listed.shape, jnp.int32), pltpu.VMEM(sums.shape, F32)),
        in_specs=[IN_SMEM] + [IN_VMEM] * 2 + [ANYWHERE] * parts + [IN_VMEM] + [ANYWHERE] * len(ties),
        out_specs=(IN_SMEM, IN_VMEM),
        input_output_aliases={3 + parts: 1},
        scratch_shapes=[
            pltpu.VMEM((parts * sums.shape[0],) + sums.shape[1:], BF16),
            pltpu.SemaphoreType.DMA((parts,)),
        ],
        compiler_params=limit(8),
        cost_estimate=SMALL,
        name="more_sums",
    )(listed, reals, imags, *sources, sums, *ties)


def apply_kernel(sums, basis, leaf00, leaf01, leaf1, leaf2, out, totals, sems):
    count = sums.shape[0]

    def store(leaf):
        return pltpu.make_async_copy(totals.at[leaf], out.at[leaf], sems.at[leaf])

    for j, own in enumerate((leaf00, leaf01)):

        @pl.loop(0, count // 8)
        def _(part):
            for i in range(4):
                o = 4 * part + i
                leaf = j * (count // 2) + o
                coef = own[o].astype(F32) + leaf1[1 - j, o].astype(F32) + leaf2[j, o].astype(F32)
                coef = coef.astype(BF16)
                far = [jnp.dot(basis[leaf, s], coef, preferred_element_type=F32) for s in range(2)]
                totals[leaf] = (sums[leaf] + jnp.concatenate(far, axis=1)).astype(BF16)
                store(leaf).start()

    for leaf in range(count):
        store(leaf).wait()


def apply_leaves(sums, basis, leaf_terms):
    count = sums.shape[0]
    leaf_terms = leaf_terms[:2] + [kept_in_vmem(a) for a in leaf_terms[2:]]
    return pl.pallas_call(
        apply_kernel,
        out_shape=jax.ShapeDtypeStruct(sums.shape, BF16),
        in_specs=[IN_VMEM] * 6,
        out_specs=IN_HBM,
        scratch_shapes=[pltpu.VMEM(sums.shape, BF16), pltpu.SemaphoreType.DMA((count,))],
        compiler_params=limit(4),
        cost_estimate=SMALL,
        name="apply_leaves",
    )(sums, basis, *leaf_terms)


def per_device(
    upper_coef, phase, cone_used, transfer, leaf_basis, charges, neighbours, near_real, near_imag
):
    columns = upper_coef.shape[-1]
    coef = upper_coef.reshape(2, 4, 2, -1, columns)
    angle = phase.transpose(1, 2, 0).reshape(ANGLES, -1)
    to_z, to_both, to_core, kept, matrices = stage(angle, cone_used.T, coef, transfer)
    transfer_core = permute(transfer, FLIP_CORE)
    from_z = permute(to_z, FLIP_Z)
    from_both = permute(to_both, FLIP_BOTH)

    below = permute(charges, UP)
    above = permute(charges, DOWN)
    neighbours = neighbours.T
    transfer_outer = permute(tied(matrices, transfer_core), FLIP_OUTER)
    reals, imags, basis, sums, beside, wrapping = own_sums(
        neighbours, near_real, near_imag, leaf_basis, charges, [transfer_core, to_z]
    )
    token = beside
    kept_matrices = tied(matrices, token)
    from_core = permute(tied(to_core, token), FLIP_CORE)
    transfer_both = permute(tied(transfer_outer, token), FLIP_CORE)
    coefs = [kept, from_core, from_z, from_both]
    moves = [kept_matrices, transfer_core, transfer_outer, transfer_both]
    crossing = crossing_charges(below, above, [token])
    token, sums = more_sums(beside, reals, imags, [below, above], sums)
    crossing = tied(crossing, from_z, from_both, from_core, transfer_both, token)
    wrapped = permute(crossing, NEXT_ROW)

    far_first, far_second = transfer_terms([2], coefs, moves, [crossing])
    up = permute(far_first, X_UP)
    down = permute(far_second, X_DOWN)
    up_first, up_second, down_first, down_second = transfer_terms([1, 3], coefs, moves)
    to_above = with_arrived(up_second, up_first, up)
    to_below = with_arrived(down_first, down_second, down)
    from_below = permute(to_above, X_UP)
    from_above = permute(to_below, X_DOWN)
    own_first, own_second = transfer_terms([0], coefs, moves, [to_above, to_below])
    _, sums = more_sums(wrapping, reals, imags, [wrapped], sums, [own_first])
    return apply_leaves(sums, basis, [own_first, own_second, from_below, from_above])


def solution(mesh):
    in_specs = (
        P("cluster", "cone", None, None),
        P("cluster", "cone", None),
        P("cluster", "cone"),
        P("cone", None, None, None),
        P(("cluster", "cone"), None, None, None),
        P(("cluster", "cone"), None, None),
        P(("cluster", "cone"), None),
        P(("cluster", "cone"), None, None, None),
        P(("cluster", "cone"), None, None, None),
    )
    out_specs = P(("cluster", "cone"), None, None)
    return jax.shard_map(
        per_device, mesh=mesh, in_specs=in_specs, out_specs=out_specs, check_vma=False
    )
```

```python
import jax
import jax.numpy as jnp
from jax import lax
from jax.experimental import pallas as pl
from jax.experimental.pallas import tpu as pltpu
from jax.sharding import PartitionSpec as P

AXES = ("cluster", "cone")
DEVICES = 128
ROW = 8
F32 = jnp.float32
BF16 = jnp.bfloat16
SMALL = pl.CostEstimate(flops=0, bytes_accessed=1024, transcendentals=0)


def moved(dx):
    return [(d, (d & ~6) | ((((d >> 1) & 3) + dx) % 4) << 1) for d in range(DEVICES)]


FLIP_CORE = [(d, d ^ 1) for d in range(DEVICES)]
FLIP_Z = [(d, d ^ 8) for d in range(DEVICES)]
FLIP_BOTH = [(d, d ^ 9) for d in range(DEVICES)]
FLIP_OUTER = [(d, d ^ 72) for d in range(DEVICES)]
X_UP = moved(1)
X_DOWN = moved(-1)
UP = [(d, d - d % ROW + (d + 1) % ROW) for d in range(DEVICES)]
DOWN = [(d, d - d % ROW + (d - 1) % ROW) for d in range(DEVICES)]
NEXT_ROW = [(d, d + ROW) for d in range(0, DEVICES - ROW, ROW)] + [
    (d, d - ROW) for d in range(2 * ROW - 1, DEVICES, ROW)
]


def permute(array, pairs):
    return lax.ppermute(array, AXES, pairs)


IN_VMEM = pl.BlockSpec(memory_space=pltpu.VMEM)
IN_HBM = pl.BlockSpec(memory_space=pltpu.HBM)
IN_SMEM = pl.BlockSpec(memory_space=pltpu.SMEM)
ANYWHERE = pl.BlockSpec(memory_space=pl.ANY)


def kept_in_hbm(array):
    return pltpu.with_memory_space_constraint(array, pltpu.HBM)


def kept_in_vmem(array):
    return pltpu.with_memory_space_constraint(array, pltpu.VMEM)


def limit(mib):
    return pltpu.CompilerParams(vmem_limit_bytes=mib << 20)


ANGLES = 16
TAIL = ANGLES


def stage_kernel(angle, used, coef, transfer, *refs):
    outs, buffers, angles, weights, sems = refs[:5], refs[5:10], refs[10], refs[11], refs[12]
    small = [pltpu.make_async_copy(angle, angles, sems.at[1, 5]), pltpu.make_async_copy(used, weights, sems.at[1, 6])]
    for copy in small:
        copy.start()
    cone = lax.axis_index("cone")
    zl, core = cone // 8, cone % 2
    sources = ((1 - zl, core), (1 - zl, 1 - core), (zl, 1 - core), (zl, core))
    rows = coef.shape[-2]
    loads = [
        [
            pltpu.make_async_copy(coef.at[z, x, c], buffers[i].at[pl.ds(x * rows, rows)], sems.at[0, i * 4 + x])
            for x in range(4)
        ]
        for i, (z, c) in enumerate(sources)
    ] + [[pltpu.make_async_copy(transfer, buffers[4], sems.at[0, 16])]]
    stores = [pltpu.make_async_copy(buffers[i], outs[i], sems.at[1, i]) for i in range(5)]
    for part in loads:
        for load in part:
            load.start()

    for copy in small:
        copy.wait()
    high = angles[...].astype(BF16)
    left = angles[...] - high.astype(F32)
    middle = left.astype(BF16)
    low = (left - middle.astype(F32)).astype(BF16)
    weight = weights[...].astype(F32)
    each = (ANGLES // 2, weight.shape[1])
    weight = jnp.concatenate([jnp.broadcast_to(weight[i : i + 1], each) for i in range(2)], axis=0)
    pieces = [piece.astype(F32) for piece in (high, middle, low)] + [weight]
    tail = jnp.concatenate(pieces, axis=1).astype(BF16)
    for buffer in buffers[:4]:
        buffer[4 * rows :, :] = tail

    for part, store in zip(loads, stores):
        for load in part:
            load.wait()
        store.start()
    for store in stores:
        store.wait()


def stage(angle, used, coef, transfer):
    part = jax.ShapeDtypeStruct((4 * coef.shape[-2] + TAIL, coef.shape[-1]), coef.dtype)
    outs = (part,) * 4 + (jax.ShapeDtypeStruct(transfer.shape, transfer.dtype),)
    return pl.pallas_call(
        stage_kernel,
        out_shape=outs,
        in_specs=[IN_HBM] * 4,
        out_specs=(IN_HBM,) * 5,
        scratch_shapes=[pltpu.VMEM(a.shape, a.dtype) for a in (*outs, angle, used)]
        + [pltpu.SemaphoreType.DMA((2, 17))],
        compiler_params=limit(5),
        cost_estimate=SMALL,
        name="stage",
    )(*[kept_in_hbm(a) for a in (angle, used, coef, transfer)])


def tied(array, *others):
    def kernel(*refs):
        del refs

    return pl.pallas_call(
        kernel,
        out_shape=jax.ShapeDtypeStruct(array.shape, array.dtype),
        in_specs=[ANYWHERE] * (1 + len(others)),
        out_specs=ANYWHERE,
        input_output_aliases={0: 0},
        compiler_params=limit(1),
        cost_estimate=SMALL,
        name="tied",
    )(array, *others)


def cross_kernel(ties, below, above, *refs):
    out, buffer, sem = refs[ties:]
    at_row = lax.rem(lax.axis_index("cone"), ROW)

    def carry(source):
        for copy in (pltpu.make_async_copy(source, buffer, sem), pltpu.make_async_copy(buffer, out, sem)):
            copy.start()
            copy.wait()

    @pl.when(at_row == 0)
    def _():
        carry(below)

    @pl.when(at_row == ROW - 1)
    def _():
        carry(above)


def crossing_charges(below, above, ties):
    def kernel(*refs):
        cross_kernel(len(ties), *refs)

    return pl.pallas_call(
        kernel,
        out_shape=jax.ShapeDtypeStruct(below.shape, below.dtype),
        in_specs=[ANYWHERE] * (2 + len(ties)),
        out_specs=ANYWHERE,
        scratch_shapes=[pltpu.VMEM(below.shape, below.dtype), pltpu.SemaphoreType.DMA],
        compiler_params=limit(3),
        cost_estimate=SMALL,
        name="crossing_charges",
    )(below, above, *ties)


def transfer_kernel(offsets, ties, *refs):
    coefs, moves, outs = refs[:4], refs[4:8], refs[8 + ties :]
    cone_index = lax.axis_index("cone")
    zl, x, core = cone_index // 8, (cone_index // 2) % 4, cone_index % 2
    size, width = outs[0].shape[1:]
    half = size // 2
    clusters = width // 4
    lanes = lax.broadcasted_iota(jnp.int32, (ANGLES, clusters), 1)
    turns = []
    for coef in coefs:
        tail = coef[coef.shape[0] - TAIL :, :].astype(F32)
        high, middle, low, weight = (tail[:, i * clusters : (i + 1) * clusters] for i in range(4))
        angle = high + middle + low
        turns.append((jnp.cos(angle) * weight, jnp.sin(angle) * weight))

    for t, offset in enumerate(offsets):
        target = (x + offset) % 4
        first = zl * 16 + target * 4 + core * 2
        columns_of = [
            [
                [
                    jnp.sum(jnp.where(lanes == first + j, part, 0.0), axis=1, keepdims=True)
                    for part in turns[source]
                ]
                for j in range(2)
            ]
            for source in range(4)
        ]
        for o in range(8):
            total = None
            for source in range(4):
                columns = []
                for j in range(2):
                    rows = []
                    for cone in range(2):
                        at = cone * 8 + o
                        cosine, sine = (column[at : at + 1] for column in columns_of[source][j])
                        start = pl.multiple_of(((target * 2 + j) * 2 + cone) * size, size)
                        real = coefs[source][pl.ds(start, half), :].astype(F32)
                        imag = coefs[source][pl.ds(start + half, half), :].astype(F32)
                        rows.append((cosine * real - sine * imag).astype(BF16))
                        rows.append((sine * real + cosine * imag).astype(BF16))
                    columns.append(jnp.concatenate(rows, axis=0))
                turned = jnp.concatenate(columns, axis=1)
                matrix = jnp.concatenate([moves[source][0, o], moves[source][1, o]], axis=1)
                term = jnp.dot(matrix, turned, preferred_element_type=F32)
                total = term if total is None else total + term
            for j in range(2):
                outs[t * 2 + j][o] = total[:, j * width : (j + 1) * width].astype(BF16)


def transfer_terms(offsets, coefs, moves, ties=()):
    out = pltpu.VMEM(moves[0].shape[1:], BF16)

    def kernel(*refs):
        transfer_kernel(offsets, len(ties), *refs)

    return pl.pallas_call(
        kernel,
        out_shape=(out,) * (2 * len(offsets)),
        in_specs=[IN_VMEM] * 8 + [ANYWHERE] * len(ties),
        out_specs=(IN_VMEM,) * (2 * len(offsets)),
        compiler_params=limit(8),
        cost_estimate=SMALL,
        name="transfer_terms",
    )(*[kept_in_vmem(a) for a in coefs], *[kept_in_vmem(a) for a in moves], *ties)


def add_kernel(left, right, arrived, *rest):
    out = rest[-1]
    for o in range(8):
        out[0, o] = left[o]
        out[1, o] = (right[o].astype(F32) + arrived[o].astype(F32)).astype(BF16)


def with_arrived(left, right, arrived, ties=()):
    return pl.pallas_call(
        add_kernel,
        out_shape=pltpu.VMEM((2,) + left.shape, BF16),
        in_specs=[IN_VMEM] * 3 + [ANYWHERE] * len(ties),
        out_specs=IN_VMEM,
        compiler_params=limit(2),
        cost_estimate=SMALL,
        name="with_arrived",
    )(left, right, kept_in_vmem(arrived), *ties)


def pair_term(real, imag, charge):
    points, columns = charge.shape[0], charge.shape[1] // 2
    both = jnp.dot(jnp.concatenate([real, imag], axis=0), charge, preferred_element_type=F32)
    first, second = both[:points], both[points:]
    return jnp.concatenate(
        [first[:, :columns] - second[:, columns:], first[:, columns:] + second[:, :columns]], axis=1
    )


GROUP = 8
PAIRS = 64
PLACES = 32


def place_of(neighbours, pair):
    count = neighbours.shape[1]
    device = lax.axis_index("cluster") * 16 + lax.axis_index("cone")
    return neighbours[pair % 4, pair // 4] - (device - 1) * count


def listed_pairs(listed, reals, imags, charges, sums, ready=None):
    length = listed[0]

    @pl.loop(0, (length + GROUP - 1) // GROUP)
    def _(group):
        places = [group * GROUP + i for i in range(GROUP)]
        entries = [listed[1 + jnp.minimum(place, length - 1)] for place in places]
        if ready is not None:
            ready(entries[-1] // (4 * PLACES))
        terms = []
        for place, entry in zip(places, entries):
            charge = charges[entry % PLACES]
            charge = jnp.where(place < length, charge, jnp.zeros_like(charge))
            leaf, n = entry // (4 * PLACES), (entry // PLACES) % 4
            terms.append((leaf, pair_term(reals[leaf, n], imags[leaf, n], charge)))
        for leaf, term in terms:
            sums[leaf] += term


LEAVES_AHEAD = 5


def own_kernel(
    ties, neighbours, near_real, near_imag, basis, own, *refs
):
    reals, imags, bases, sums, beside, wrapping, inner, charges, loaded, sems, other_sems = refs[ties:]
    count = own.shape[0]
    load_charges = pltpu.make_async_copy(own, charges, other_sems.at[0])
    load_basis = pltpu.make_async_copy(basis, bases, other_sems.at[1])

    def loads(leaf):
        return (
            pltpu.make_async_copy(near_real.at[leaf], reals.at[leaf], sems.at[0, leaf]),
            pltpu.make_async_copy(near_imag.at[leaf], imags.at[leaf], sems.at[1, leaf]),
        )

    load_charges.start()
    for leaf in range(LEAVES_AHEAD):
        for copy in loads(leaf):
            copy.start()

    at_row = lax.rem(lax.axis_index("cone"), ROW)
    for listed in (inner, beside, wrapping):
        listed[0] = 0

    @pl.loop(0, count * 4)
    def _(pair):
        at = place_of(neighbours, pair)
        low, high = at < count, at >= 2 * count
        wraps = (low & (at_row == 0)) | (high & (at_row == ROW - 1))

        inside = lax.rem(at, count)

        def put(listed, charges_at):
            length = listed[0] + 1
            listed[0] = length
            listed[length] = pair * PLACES + charges_at

        @pl.when(jnp.logical_not(low | high))
        def _():
            put(inner, inside)

        @pl.when(wraps)
        def _():
            put(wrapping, inside)

        @pl.when((low | high) & jnp.logical_not(wraps))
        def _():
            put(beside, jnp.where(low, inside, inside + count))

    loaded[0] = 0

    @pl.loop(0, count)
    def _(leaf):
        sums[leaf] = jnp.zeros(sums.shape[1:], F32)

    load_charges.wait()

    def ready(leaf):
        @pl.loop(loaded[0], leaf + 1)
        def _(waited):
            for copy in loads(waited):
                copy.wait()

            @pl.when(waited + LEAVES_AHEAD < count)
            def _():
                for copy in loads(waited + LEAVES_AHEAD):
                    copy.start()

        loaded[0] = jnp.maximum(loaded[0], leaf + 1)

    listed_pairs(inner, reals, imags, charges, sums, ready)
    load_basis.start()
    ready(count - 1)
    load_basis.wait()


def own_sums(neighbours, near_real, near_imag, basis, own, ties):
    count = own.shape[0]
    pairs = jax.ShapeDtypeStruct((1 + PAIRS,), jnp.int32)

    def kernel(*refs):
        own_kernel(len(ties), *refs)

    return pl.pallas_call(
        kernel,
        out_shape=(
            pltpu.VMEM(near_real.shape, BF16),
            pltpu.VMEM(near_imag.shape, BF16),
            pltpu.VMEM(basis.shape, BF16),
            pltpu.VMEM(own.shape, F32),
            pairs,
            pairs,
        ),
        in_specs=[IN_SMEM] + [IN_HBM] * 4 + [ANYWHERE] * len(ties),
        out_specs=(IN_VMEM,) * 4 + (IN_SMEM,) * 2,
        scratch_shapes=[
            pltpu.SMEM(pairs.shape, jnp.int32),
            pltpu.VMEM(own.shape, BF16),
            pltpu.SMEM((1,), jnp.int32),
            pltpu.SemaphoreType.DMA((2, count)),
            pltpu.SemaphoreType.DMA((2,)),
        ],
        compiler_params=limit(6),
        cost_estimate=SMALL,
        name="own_sums",
    )(neighbours, *[kept_in_hbm(a) for a in (near_real, near_imag, basis, own)], *ties)


def more_kernel(parts, ties, listed, reals, imags, *refs):
    sources = refs[:parts]
    token, sums, charges, sems = refs[parts + 1 + ties :]
    count = reals.shape[0]
    token[0] = 0

    @pl.when(listed[0] > 0)
    def _():
        copies = [
            pltpu.make_async_copy(source, charges.at[pl.ds(i * count, count)], sems.at[i])
            for i, source in enumerate(sources)
        ]
        for copy in copies:
            copy.start()
        for copy in copies:
            copy.wait()

    listed_pairs(listed, reals, imags, charges, sums)


def more_sums(listed, reals, imags, sources, sums, ties=()):
    parts = len(sources)

    def kernel(*refs):
        more_kernel(parts, len(ties), *refs)

    return pl.pallas_call(
        kernel,
        out_shape=(jax.ShapeDtypeStruct(listed.shape, jnp.int32), pltpu.VMEM(sums.shape, F32)),
        in_specs=[IN_SMEM] + [IN_VMEM] * 2 + [ANYWHERE] * parts + [IN_VMEM] + [ANYWHERE] * len(ties),
        out_specs=(IN_SMEM, IN_VMEM),
        input_output_aliases={3 + parts: 1},
        scratch_shapes=[
            pltpu.VMEM((parts * sums.shape[0],) + sums.shape[1:], BF16),
            pltpu.SemaphoreType.DMA((parts,)),
        ],
        compiler_params=limit(8),
        cost_estimate=SMALL,
        name="more_sums",
    )(listed, reals, imags, *sources, sums, *ties)


def apply_kernel(sums, basis, leaf00, leaf01, leaf1, leaf2, out, totals, sems):
    count = sums.shape[0]

    def store(leaf):
        return pltpu.make_async_copy(totals.at[leaf], out.at[leaf], sems.at[leaf])

    for j, own in enumerate((leaf00, leaf01)):

        for o in range(count // 2):
            leaf = j * (count // 2) + o
            coef = own[o].astype(F32) + leaf1[1 - j, o].astype(F32) + leaf2[j, o].astype(F32)
            coef = coef.astype(BF16)
            far = [jnp.dot(basis[leaf, s], coef, preferred_element_type=F32) for s in range(2)]
            totals[leaf] = (sums[leaf] + jnp.concatenate(far, axis=1)).astype(BF16)
            store(leaf).start()

    for leaf in range(count):
        store(leaf).wait()


def apply_leaves(sums, basis, leaf_terms):
    count = sums.shape[0]
    leaf_terms = leaf_terms[:2] + [kept_in_vmem(a) for a in leaf_terms[2:]]
    return pl.pallas_call(
        apply_kernel,
        out_shape=jax.ShapeDtypeStruct(sums.shape, BF16),
        in_specs=[IN_VMEM] * 6,
        out_specs=IN_HBM,
        scratch_shapes=[pltpu.VMEM(sums.shape, BF16), pltpu.SemaphoreType.DMA((count,))],
        compiler_params=limit(4),
        cost_estimate=SMALL,
        name="apply_leaves",
    )(sums, basis, *leaf_terms)


def per_device(
    upper_coef, phase, cone_used, transfer, leaf_basis, charges, neighbours, near_real, near_imag
):
    columns = upper_coef.shape[-1]
    coef = upper_coef.reshape(2, 4, 2, -1, columns)
    angle = phase.transpose(1, 2, 0).reshape(ANGLES, -1)
    to_z, to_both, to_core, kept, matrices = stage(angle, cone_used.T, coef, transfer)
    transfer_core = permute(transfer, FLIP_CORE)
    from_z = permute(to_z, FLIP_Z)
    from_both = permute(to_both, FLIP_BOTH)

    below = permute(charges, UP)
    above = permute(charges, DOWN)
    neighbours = neighbours.T
    transfer_outer = permute(tied(matrices, transfer_core), FLIP_OUTER)
    reals, imags, basis, sums, beside, wrapping = own_sums(
        neighbours, near_real, near_imag, leaf_basis, charges, [transfer_core, to_z]
    )
    token = beside
    kept_matrices = tied(matrices, token)
    from_core = permute(tied(to_core, token), FLIP_CORE)
    transfer_both = permute(tied(transfer_outer, token), FLIP_CORE)
    coefs = [kept, from_core, from_z, from_both]
    moves = [kept_matrices, transfer_core, transfer_outer, transfer_both]
    crossing = crossing_charges(below, above, [token])
    token, sums = more_sums(beside, reals, imags, [below, above], sums)
    crossing = tied(crossing, from_z, from_both, from_core, transfer_both, token)
    wrapped = permute(crossing, NEXT_ROW)

    far_first, far_second = transfer_terms([2], coefs, moves, [crossing])
    up = permute(far_first, X_UP)
    down = permute(far_second, X_DOWN)
    up_first, up_second, down_first, down_second = transfer_terms([1, 3], coefs, moves)
    to_above = with_arrived(up_second, up_first, up)
    to_below = with_arrived(down_first, down_second, down)
    from_below = permute(to_above, X_UP)
    from_above = permute(to_below, X_DOWN)
    own_first, own_second = transfer_terms([0], coefs, moves, [to_above, to_below])
    _, sums = more_sums(wrapping, reals, imags, [wrapped], sums, [own_first])
    return apply_leaves(sums, basis, [own_first, own_second, from_below, from_above])


def solution(mesh):
    in_specs = (
        P("cluster", "cone", None, None),
        P("cluster", "cone", None),
        P("cluster", "cone"),
        P("cone", None, None, None),
        P(("cluster", "cone"), None, None, None),
        P(("cluster", "cone"), None, None),
        P(("cluster", "cone"), None),
        P(("cluster", "cone"), None, None, None),
        P(("cluster", "cone"), None, None, None),
    )
    out_specs = P(("cluster", "cone"), None, None)
    return jax.shard_map(
        per_device, mesh=mesh, in_specs=in_specs, out_specs=out_specs, check_vma=False
    )
```
